256 devices in a mesh: dp: 16 (over z, core), mp: 16 (over y, x).
Axes of the slice: x: 4, y: 4, z: 8, core: 2. Of those that a mesh axis runs over, the one named last changes fastest.
Arguments:
- residual: bfloat16 [2048, 4096], P('dp'), may hold values from -6 to 6
- norm_gain: float32 [4096], replicated, may hold values from 0.5 to 1.5
- head_weight: bfloat16 [4096, 38912], P('dp', 'mp'), may hold values from -8 to 8
- token_ids: int32 [2048], P('dp'), may hold values from 0 to 38911
- old_logp: float32 [2048], P('dp'), may hold values from -40 to 0
- advantages: float32 [2048], P('dp'), may hold values from -4 to 4
- resp_mask: int32 [2048], P('dp'), may hold values 0 or 1
- routes: int32 [2048, 8], P('dp'), may hold values from 0 to 63, all different within a row; in each aligned block of 128 rows (0 to 127, 128 to 255, ...) at most 32 rows name the same one
- combine_weights: bfloat16 [2048, 8], P('dp'), may hold values from 0.019897461 to 0.29882812
- expert_acts: bfloat16 [64, 16, 32, 1536], P('mp', 'dp'), may hold values from -6 to 6
- down_weight: bfloat16 [64, 1536, 4096], P('mp', None, 'dp'), may hold values from -0.15625 to 0.15625
Outputs:
- resid_grad: float32 [2048, 4096], P('dp', 'mp')
- down_grad: bfloat16 [64, 1536, 4096], P('mp', None, 'dp')
- gate_grad: float32 [2048, 8], P('dp')
The draws below stay inside these ranges and needn't reach their ends.
Inputs may be any that keep to these rules, and one draw needn't show every extreme that they name: `routes`: each row names 8 different experts. Among the 128 rows of one data group no expert is named more than 32 times, a bound that some block reaches.
All inputs are finite; a program needn't handle non-finite values. No bound on the sum of `resp_mask` on one device may be relied on, other than what follows from the above.
Results may differ from the reference program's by a relative error of at most 0.012.
The reference program's roundings to bfloat16 on the way (of `normed`, `logit_grad`, `stream_grad`, `slot_rows` and `weighted`) count: a program that leaves them out, or rounds other values in their place, can miss the bound.
Values may be sent and summed in bfloat16 or wider, within the bound.
No kernel may reach another device: no remote copies, remote signals or barrier semaphores. Data moves between devices by JAX's collectives and lax.ppermute only.
A program may use at most 128 MiB of HBM per device.

```python
import math
import jax
import jax.numpy as jnp
import numpy as np
from jax import lax

D = 4096
FF = 1536
TOPK = 8
TOK = 128
TOKENS = 2048
VOCAB = 38912
EXPERTS = 64
CAP = 32
N_DP = 16


def draw_head_weight(key, part):
    key = jax.random.fold_in(key, 11)
    base_key = jax.random.fold_in(key, 0)
    values = jax.random.normal(base_key, (D, VOCAB), jnp.float32) * (3.0 / math.sqrt(D))
    return jnp.clip(values, -8.0, 8.0).astype(jnp.bfloat16)


def draw_old_logp(key, part):
    key = jax.random.fold_in(key, 23)
    center = -(math.log(VOCAB) + 4.5)
    values = center + 1.5 * jax.random.normal(key, (TOKENS,), jnp.float32)
    return jnp.clip(values, -40.0, -0.01)


def with_ends(array, key, least, high):
    dims = array.shape
    spot = [jax.random.randint(jax.random.fold_in(key, axis), (), 0, dims[axis]) for axis in range(len(dims))]
    array = array.at[tuple(spot)].set(least)
    longest = dims.index(max(dims))
    spot[longest] = (spot[longest] + 1) % dims[longest]
    return array.at[tuple(spot)].set(high)


def block_scale(own_key, shape, cuts, low, high):
    def one(dim, shards_of):
        heights = jax.random.uniform(jax.random.fold_in(jax.random.fold_in(own_key, 6), dim), (shards_of,), jnp.float32, low / len(cuts), high / len(cuts))
        return jnp.repeat(jnp.exp(heights), shape[dim] // shards_of).reshape((-1,) + (1,) * (len(shape) - dim - 1))

    loudness = one(*cuts[0])
    for cut in cuts[1:]:
        loudness = loudness * one(*cut)
    return loudness


def assign_block(stream_key, own, number, rows, count, top, reach, skew):
    ranking = jax.random.permutation(stream_key, count)
    packed, usual = portions_of(count, rows * top, reach, skew, True), portions_of(count, rows * top, reach, skew, False)
    places = jnp.arange(count)

    def named(lengths, offset_by):
        used = int((lengths > 0).sum())
        fixed = max(1, used // 4)
        moved = fixed + (places - fixed + offset_by * (used - fixed)) % max(1, count - fixed)
        return jnp.zeros((count,), jnp.int32).at[ranking[jnp.where(places < fixed, places, moved)]].set(jnp.asarray(lengths, jnp.int32))

    lengths = jnp.where(number % 4 == 0, named(packed, number // 4), named(usual, number - number // 4 - 1))
    mixed = jax.random.permutation(jax.random.fold_in(own, 3), count)
    giver, taker = mixed[0:count // 2 * 2:2], mixed[1:count // 2 * 2:2]
    room = jnp.minimum(lengths[giver] - 1, reach - lengths[taker]) // 2
    room = jnp.where((giver == ranking[0]) | (taker == ranking[0]) | (lengths[taker] == 0), 0, jnp.maximum(room, 0))
    moved = jax.random.randint(jax.random.fold_in(own, 4), (count // 2,), 0, 1 << 20) % (room + 1)
    lengths = lengths.at[giver].add(-moved).at[taker].add(moved)
    labels = jnp.searchsorted(jnp.cumsum(lengths), jnp.arange(rows * top), side="right").astype(jnp.int32)
    table = labels.reshape(top, rows).T
    table = table[jax.random.permutation(jax.random.fold_in(own, 1), rows)]
    offset_by = jax.random.randint(jax.random.fold_in(own, 2), (rows, 1), 0, top)
    return jnp.take_along_axis(table, (jnp.arange(top)[None, :] + offset_by) % top, axis=1)


def portions_of(count, total, reach, lean, full):
    portions = [(1 << 20) // math.isqrt(standing ** lean) + 1 for standing in range(1, count + 1)]
    largest = reach if full else min(reach, max(-(-total // count), total * portions[0] // sum(portions)))
    least = 1 if total - largest >= count - 1 else 0
    counts, rest = [largest] + [least] * (count - 1), total - largest - least * (count - 1)
    while rest > 0:
        candidates = [i for i in range(1, count) if counts[i] < largest] or [i for i in range(1, count) if counts[i] < reach]
        pool, remaining = sum([portions[i] for i in candidates]), rest
        for i in candidates:
            extra = min(reach - counts[i], max(1, remaining * portions[i] // pool), rest)
            counts[i] = counts[i] + extra
            rest = rest - extra
    return np.array(counts)


def bell_draw(own_key, shape, scale, bound, shards=(), kind=jnp.bfloat16):
    result = scale * jax.random.normal(own_key, shape, jnp.float32)
    if shards:
        result = result * block_scale(own_key, shape, shards, -0.22, 0.18)
    return jnp.clip(result, -bound, bound).astype(kind)


def setup_inputs(seed: int = 0) -> dict:
    key_of = jax.random.split(jax.random.key(seed), 12)
    residual = bell_draw(key_of[0], (TOKENS, D), 1.0, 6.0, ((0, 16),))
    norm_gain = jnp.clip(1.0 + 0.1 * jax.random.normal(key_of[1], (D,), jnp.float32), 0.5, 1.5)
    head_weight = draw_head_weight(jax.random.fold_in(key_of[11], 71), 0)
    token_ids = with_ends(jax.random.randint(key_of[3], (TOKENS,), 0, VOCAB), jax.random.fold_in(key_of[3], 1), 0, VOCAB - 1).astype(jnp.int32)
    old_logp = draw_old_logp(jax.random.fold_in(key_of[11], 71), 0)
    advantages = bell_draw(key_of[5], (TOKENS,), 1.0, 4.0, ((0, 16),), jnp.float32)
    resp_mask = with_ends((jax.random.randint(key_of[6], (TOKENS,), 0, 4) < 3).astype(jnp.int32), jax.random.fold_in(key_of[6], 1), 0, 1)
    routes_keys = jax.random.split(jax.random.fold_in(key_of[7], 1), TOKENS // TOK)
    routes_turns = jax.random.permutation(jax.random.fold_in(key_of[7], 3), TOKENS // TOK)
    routes = jax.vmap(lambda own, number: assign_block(jax.random.fold_in(key_of[7], 2), own, number, TOK, EXPERTS, TOPK, CAP, 2))(routes_keys, routes_turns).reshape((TOKENS, TOPK))
    combine_weights = jnp.clip(0.019897461 + 0.27893066 * jax.random.uniform(key_of[8], (TOKENS, TOPK), jnp.float32) ** block_scale(key_of[8], (TOKENS, TOPK), ((0, 16),), -0.2, 0.2), 0.019897461, 0.29882812).astype(jnp.bfloat16)
    expert_acts = bell_draw(key_of[9], (EXPERTS, N_DP, CAP, FF), 1.0, 6.0, ((0, 16), (1, 16)))
    down_weight = bell_draw(key_of[10], (EXPERTS, FF, D), FF ** -0.5, 0.15625, ((0, 16), (2, 16)))
    return dict(residual=residual, norm_gain=norm_gain, head_weight=head_weight, token_ids=token_ids, old_logp=old_logp, advantages=advantages, resp_mask=resp_mask, routes=routes, combine_weights=combine_weights, expert_acts=expert_acts, down_weight=down_weight)


clip_low = 0.8
clip_high = 1.2
norm_eps = 1e-06

def token_coef(picked, row_top, row_total, old_group, adv_group, mask_group):
    logp = picked - row_top - jnp.log(row_total)
    prob_ratio = jnp.exp(logp - old_group)
    return -jnp.clip(prob_ratio, clip_low, clip_high) * adv_group * mask_group.astype(jnp.float32)

def head_group(inputs, head_weight):
    normed, ids_group, old_group, adv_group, mask_group = inputs
    logits = jnp.dot(normed, head_weight, preferred_element_type=jnp.float32)
    row_top = lax.optimization_barrier(jnp.max(logits, axis=1))
    shifted = jnp.exp(logits - row_top[:, None])
    row_total = lax.optimization_barrier(jnp.sum(shifted, axis=1))
    column = jnp.arange(logits.shape[1], dtype=jnp.int32)
    onehot = column[None, :] == ids_group[:, None]
    picked = lax.optimization_barrier(jnp.sum(jnp.where(onehot, logits, 0.0), axis=1))
    weight_row = token_coef(picked, row_top, row_total, old_group, adv_group, mask_group)
    logit_grad = (weight_row[:, None] * (onehot.astype(jnp.float32) - shifted / row_total[:, None])).astype(jnp.bfloat16)
    return lax.dot_general(logit_grad, head_weight, (((1,), (1,)), ((), ())), preferred_element_type=jnp.float32)

def reference(residual, norm_gain, head_weight, token_ids, old_logp, advantages, resp_mask, routes, combine_weights, expert_acts, down_weight):
    stream = residual.astype(jnp.float32)
    inv_rms = lax.rsqrt(lax.optimization_barrier(jnp.mean(stream * stream, axis=1, keepdims=True)) + norm_eps)
    normed = (stream * inv_rms * norm_gain[None, :]).astype(jnp.bfloat16)
    grouped = (normed.reshape(N_DP, TOK, D), token_ids.reshape(N_DP, TOK), old_logp.reshape(N_DP, TOK), advantages.reshape(N_DP, TOK), resp_mask.reshape(N_DP, TOK))
    hidden_grad = lax.map(lambda inputs: head_group(inputs, head_weight), grouped).reshape(TOKENS, D)
    scaled_grad = norm_gain[None, :] * hidden_grad
    unit = stream * inv_rms
    inner = lax.optimization_barrier(jnp.sum(unit * scaled_grad, axis=1, keepdims=True)) / D
    resid_grad = inv_rms * (scaled_grad - unit * inner)
    stream_grad = lax.optimization_barrier(resid_grad.astype(jnp.bfloat16))
    grad_rows = stream_grad.astype(jnp.float32).reshape(N_DP, TOK, D)
    route_groups = routes.reshape(N_DP, TOK, TOPK)
    weight_groups = combine_weights.astype(jnp.float32).reshape(N_DP, TOK, TOPK)
    slot_ids = jnp.arange(CAP, dtype=jnp.int32)

    def expert_step(gate_acc, expert):
        hit_routes = route_groups == expert
        hit_token = lax.optimization_barrier(jnp.sum(hit_routes.astype(jnp.int32), axis=2))
        before = jnp.cumsum(hit_token, axis=1) - hit_token
        matches = ((hit_token[:, None, :] == 1) & (before[:, None, :] == slot_ids[None, :, None])).astype(jnp.float32)
        slot_rows = jnp.einsum('gst,gtd->gsd', matches, grad_rows, precision=lax.Precision.HIGHEST)
        weight_token = lax.optimization_barrier(jnp.sum(jnp.where(hit_routes, weight_groups, 0.0), axis=2))
        slot_weight = jnp.einsum('gst,gt->gs', matches, weight_token, precision=lax.Precision.HIGHEST)
        acts = lax.dynamic_index_in_dim(expert_acts, expert, 0, keepdims=False).reshape(N_DP * CAP, FF)
        weight_down = lax.dynamic_index_in_dim(down_weight, expert, 0, keepdims=False)
        proj = jnp.dot(acts, weight_down, preferred_element_type=jnp.float32).reshape(N_DP, CAP, D)
        slot_gate = lax.optimization_barrier(jnp.sum(slot_rows * proj, axis=2))
        weighted = (slot_weight[:, :, None] * slot_rows).astype(jnp.bfloat16)
        grad_expert = lax.dot_general(acts, weighted.reshape(N_DP * CAP, D), (((0,), (0,)), ((), ())), preferred_element_type=jnp.float32).astype(jnp.bfloat16)
        per_token = jnp.einsum('gst,gs->gt', matches, slot_gate, precision=lax.Precision.HIGHEST)
        gate_acc = gate_acc + jnp.where(hit_routes, per_token[:, :, None], 0.0)
        return (gate_acc, grad_expert)
    gate_start = jnp.zeros((N_DP, TOK, TOPK), jnp.float32)
    gate_grad, down_grad = lax.scan(expert_step, gate_start, jnp.arange(EXPERTS, dtype=jnp.int32))
    return (resid_grad, down_grad, gate_grad.reshape(TOKENS, TOPK))
```

```python
import functools

import jax
import jax.numpy as jnp
from jax import lax
from jax.experimental import pallas as pl
from jax.experimental.pallas import tpu as pltpu
from jax.sharding import PartitionSpec as P

clip_low = 0.8
clip_high = 1.2
norm_eps = 1e-06
f32 = jnp.float32
bf16 = jnp.bfloat16
lanes = 128


def z_shift(step, nz):
    return [(2 * z + c, 2 * ((z + step) % nz) + c) for z in range(nz) for c in range(2)]


def core_swap(nz):
    return [(2 * z + c, 2 * z + 1 - c) for z in range(nz) for c in range(2)]


def z_ring(block, nz):
    ahead = back = block
    pieces = [(0, 0, block)]
    for step in range(1, nz // 2):
        ahead = lax.ppermute(ahead, "dp", z_shift(1, nz))
        back = lax.ppermute(back, "dp", z_shift(-1, nz))
        pieces += [(nz - step, 0, ahead), (step, 0, back)]
    half = block.shape[0] // 2
    pieces += [
        (nz // 2, 0, lax.ppermute(ahead[:half], "dp", z_shift(1, nz))),
        (nz // 2, half, lax.ppermute(back[half:], "dp", z_shift(-1, nz))),
    ]
    return pieces


def proj_kernel(acts_ref, down_ref, proj_ref):
    groups, _, slots, wide = acts_ref.shape
    width = down_ref.shape[1]
    acts = acts_ref[:, 0, :, :width].reshape(groups * slots, width)
    out = jnp.dot(acts, down_ref[0], preferred_element_type=f32)
    proj_ref[...] = out.reshape(proj_ref.shape)


def slot_kernel(place_ref, group_ref, side_ref, rows_ref, proj_ref, weighted_ref, gate_ref):
    per_expert, slots, _ = side_ref.shape[1:]
    side = side_ref[0].reshape(per_expert * slots, lanes).astype(f32)
    weight = side[:, 0:1]
    token = side[:, 1:2]
    tokens = rows_ref.shape[1]
    column = lax.broadcasted_iota(jnp.int32, (per_expert * slots, tokens), 1).astype(f32)
    match = jnp.where(column == token, 1.0, 0.0).astype(bf16)
    rows = jnp.dot(match, rows_ref[0], preferred_element_type=f32)
    proj = proj_ref[:, 0].reshape(rows.shape)
    ones = jnp.ones((8, rows.shape[1]), f32)
    gate_ref[0] = lax.dot_general(
        ones, rows * proj, (((1,), (1,)), ((), ())),
        precision=lax.Precision.HIGHEST, preferred_element_type=f32,
    )
    weighted_ref[:, 0] = (weight * rows).astype(bf16).reshape(per_expert, slots, rows.shape[1])


def down_kernel(acts_ref, weighted_ref, out_ref):
    groups, _, slots, wide = acts_ref.shape
    width = out_ref.shape[1]
    acts = acts_ref[:, 0, :, :width].reshape(groups * slots, width)
    weighted = weighted_ref[0].reshape(groups * slots, weighted_ref.shape[3])
    out_ref[0] = lax.dot_general(
        acts, weighted, (((0,), (0,)), ((), ())), preferred_element_type=f32
    ).astype(bf16)


def local(
    residual,
    norm_gain,
    head_weight,
    token_ids,
    old_logp,
    advantages,
    resp_mask,
    routes,
    combine_weights,
    expert_acts,
    down_weight,
):
    tokens, model_width = residual.shape
    block, vocab_dev = head_weight.shape
    per_expert, _, capacity, hidden_width = expert_acts.shape
    dp_count = lax.axis_size("dp")
    mp_count = lax.axis_size("mp")
    nz = dp_count // 2
    dp_index = lax.axis_index("dp")
    mp_index = lax.axis_index("mp")
    z_index, core = dp_index // 2, dp_index % 2
    experts_all = per_expert * mp_count
    swap = functools.partial(lax.ppermute, axis_name="dp", perm=core_swap(nz))

    head_pieces = z_ring(head_weight, nz)

    stream = residual.astype(f32)
    inv_rms = lax.rsqrt(jnp.mean(stream * stream, axis=1, keepdims=True) + norm_eps)
    normed = (stream * inv_rms * norm_gain[None, :]).astype(bf16)
    by_block = normed.reshape(tokens, nz, 2, block).transpose(2, 1, 0, 3)
    mine = lax.dynamic_index_in_dim(by_block, core, 0, keepdims=False)
    theirs = lax.dynamic_index_in_dim(by_block, 1 - core, 0, keepdims=False)
    chip_normed = jnp.concatenate([mine, swap(theirs)], axis=1)

    expert_ids = jnp.arange(experts_all, dtype=jnp.int32)
    hit_routes = routes[:, :, None] == expert_ids[None, None, :]
    hit_token = jnp.sum(hit_routes.astype(jnp.int32), axis=1)
    before = jnp.cumsum(hit_token, axis=0) - hit_token
    slot_ids = jnp.arange(capacity, dtype=jnp.int32)
    matches = (hit_token.T[:, None, :] == 1) & (before.T[:, None, :] == slot_ids[None, :, None])
    weight_token = jnp.sum(
        jnp.where(hit_routes, combine_weights[:, :, None].astype(f32), 0.0), axis=1
    )
    first_expert = mp_index * per_expert
    own_matches = lax.dynamic_slice_in_dim(matches, first_expert, per_expert, 0)
    own_weights = lax.dynamic_slice_in_dim(weight_token, first_expert, per_expert, 1)
    slot_weight = jnp.sum(jnp.where(own_matches, own_weights.T[:, None, :], 0.0), axis=2)
    token_numbers = jnp.arange(tokens, dtype=jnp.int32)
    slot_token = jnp.sum(jnp.where(own_matches, token_numbers[None, None, :] + 1, 0), axis=2) - 1
    lane = jnp.arange(lanes, dtype=jnp.int32)
    side = jnp.where(
        lane == 0,
        slot_weight[:, :, None],
        jnp.where(lane == 1, slot_token.astype(f32)[:, :, None], 0.0),
    ).astype(bf16)
    acts_block = jnp.concatenate([expert_acts[:, 0], side], axis=2)

    partial = jnp.zeros((2 * tokens, vocab_dev), f32)
    for offset, first, piece in head_pieces:
        features = lax.dynamic_index_in_dim(
            chip_normed, lax.rem(z_index + offset, nz), 0, keepdims=False
        )[:, first : first + piece.shape[0]]
        partial = partial + jnp.dot(features, piece, preferred_element_type=f32)
    logits = partial[:tokens] + swap(partial[tokens:])

    local_ids = token_ids - mp_index * vocab_dev
    column = jnp.arange(vocab_dev, dtype=jnp.int32)
    onehot = column[None, :] == local_ids[:, None]
    local_top = jnp.max(logits, axis=1)
    local_exp = jnp.exp(logits - local_top[:, None])
    local_total = jnp.sum(local_exp, axis=1)
    local_mean = jnp.sum(local_exp * logits, axis=1)
    local_picked = jnp.sum(jnp.where(onehot, logits, 0.0), axis=1)
    stats = jnp.stack([local_top, local_total, local_mean, local_picked])
    stats = lax.all_to_all(
        jnp.broadcast_to(stats[None], (mp_count, 4, tokens)), "mp", 0, 0, tiled=True
    )
    row_top = jnp.max(stats[:, 0], axis=0)
    rescale = jnp.exp(stats[:, 0] - row_top[None])
    row_total = jnp.sum(stats[:, 1] * rescale, axis=0)
    mean_logit = jnp.sum(stats[:, 2] * rescale, axis=0) / row_total
    picked = jnp.sum(stats[:, 3], axis=0)

    logp = picked - row_top - jnp.log(row_total)
    prob_ratio = jnp.exp(logp - old_logp)
    weight_row = -jnp.clip(prob_ratio, clip_low, clip_high) * advantages * resp_mask.astype(f32)
    inner = weight_row * (picked - mean_logit) / model_width
    logit_grad = (
        weight_row[:, None]
        * (onehot.astype(f32) - jnp.exp(logits - row_top[:, None]) / row_total[:, None])
    ).astype(bf16)
    chip_grad = jnp.concatenate([logit_grad, swap(logit_grad)], axis=0)

    parts = []
    for offset, first, piece in head_pieces:
        parts.append(
            lax.dot_general(
                chip_grad, piece, (((1,), (1,)), ((), ())), preferred_element_type=f32
            )
        )
    parts = parts[:1] + parts[2:-2:2] + [jnp.concatenate(parts[-2:], axis=1)] + parts[-4:0:-2]
    by_offset = jnp.stack(parts)
    hidden = jnp.roll(by_offset, z_index, axis=0)
    own_part, other_part = hidden[:, :tokens], swap(hidden[:, tokens:])
    hidden = jnp.where(
        core == 0,
        jnp.stack([own_part, other_part], axis=1),
        jnp.stack([other_part, own_part], axis=1),
    ).reshape(mp_count, tokens, block)
    hidden_grad = jnp.sum(lax.all_to_all(hidden, "mp", 0, 0, tiled=True), axis=0)

    my_stream = lax.dynamic_slice_in_dim(stream, mp_index * block, block, 1)
    my_gain = lax.dynamic_slice_in_dim(norm_gain, mp_index * block, block, 0)
    scaled_grad = my_gain[None, :] * hidden_grad
    resid_grad = inv_rms * (scaled_grad - my_stream * inv_rms * inner[:, None])
    stream_grad = resid_grad.astype(bf16)

    turned = lax.ppermute(
        stream_grad,
        ("dp", "mp"),
        [(p * mp_count + q, q * mp_count + p) for p in range(dp_count) for q in range(mp_count)],
    )
    all_rows = lax.all_to_all(
        jnp.broadcast_to(turned[None], (mp_count, tokens, block)), "mp", 0, 0, tiled=True
    )

    pieces = z_ring(acts_block, nz)
    acts_list = [p for _, _, p in pieces[:-2]] + [jnp.concatenate([pieces[-2][2], pieces[-1][2]], axis=0)]
    offsets = [o for o, _, _ in pieces[:-1]]
    acts_own = jnp.stack(acts_list)
    acts_all = jnp.concatenate([acts_own, swap(acts_own)], axis=0)
    offsets = jnp.array(offsets, jnp.int32)
    z_of = lax.rem(z_index + offsets, nz)
    group_of = jnp.concatenate([2 * z_of + core, 2 * z_of + 1 - core]).astype(jnp.int32)

    wide = hidden_width + lanes
    proj = pl.pallas_call(
        proj_kernel,
        grid=(per_expert,),
        in_specs=[
            pl.BlockSpec((dp_count, 1, capacity, wide), lambda e: (0, e, 0, 0)),
            pl.BlockSpec((1, hidden_width, block), lambda e: (e, 0, 0)),
        ],
        out_specs=pl.BlockSpec((1, dp_count, capacity, block), lambda e: (e, 0, 0, 0)),
        out_shape=jax.ShapeDtypeStruct((per_expert, dp_count, capacity, block), f32),
        compiler_params=pltpu.CompilerParams(vmem_limit_bytes=32 * 1024 * 1024),
    )(acts_all, down_weight)
    weighted, gate = pl.pallas_call(
        slot_kernel,
        grid_spec=pltpu.PrefetchScalarGridSpec(
            num_scalar_prefetch=2,
            grid=(dp_count,),
            in_specs=[
                pl.BlockSpec(
                    (1, per_expert, capacity, lanes),
                    lambda n, place, group: (n, 0, 0, hidden_width // lanes),
                ),
                pl.BlockSpec((1, tokens, block), lambda n, place, group: (place[n], 0, 0)),
                pl.BlockSpec((per_expert, 1, capacity, block), lambda n, place, group: (0, n, 0, 0)),
            ],
            out_specs=[
                pl.BlockSpec((per_expert, 1, capacity, block), lambda n, place, group: (0, n, 0, 0)),
                pl.BlockSpec((1, 8, per_expert * capacity), lambda n, place, group: (group[n], 0, 0)),
            ],
        ),
        out_shape=[
            jax.ShapeDtypeStruct((per_expert, dp_count, capacity, block), bf16),
            jax.ShapeDtypeStruct((dp_count, 8, per_expert * capacity), f32),
        ],
    )(group_of, group_of, acts_all, all_rows, proj)
    down_grad = pl.pallas_call(
        down_kernel,
        grid=(per_expert,),
        in_specs=[
            pl.BlockSpec((dp_count, 1, capacity, wide), lambda e: (0, e, 0, 0)),
            pl.BlockSpec((1, dp_count, capacity, block), lambda e: (e, 0, 0, 0)),
        ],
        out_specs=pl.BlockSpec((1, hidden_width, block), lambda e: (e, 0, 0)),
        out_shape=jax.ShapeDtypeStruct((per_expert, hidden_width, block), bf16),
        compiler_params=pltpu.CompilerParams(vmem_limit_bytes=32 * 1024 * 1024),
    )(acts_all, weighted)

    group_gate = jnp.sum(
        lax.all_to_all(gate[:, :1, :], "dp", 0, 0, tiled=True), axis=0, keepdims=True
    )
    slot_gate = lax.all_to_all(
        jnp.broadcast_to(group_gate, (mp_count, 1, per_expert * capacity)), "mp", 0, 0, tiled=True
    ).reshape(experts_all, capacity)
    per_token = jnp.sum(jnp.where(matches, slot_gate[:, :, None], 0.0), axis=1)
    gate_grad = jnp.sum(jnp.where(hit_routes, per_token.T[:, None, :], 0.0), axis=2)
    return (resid_grad, down_grad, gate_grad)


def solution(mesh):
    placed = (
        P("dp", None),
        P(),
        P("dp", "mp"),
        P("dp"),
        P("dp"),
        P("dp"),
        P("dp"),
        P("dp", None),
        P("dp", None),
        P("mp", "dp", None, None),
        P("mp", None, "dp"),
    )
    return jax.shard_map(
        local,
        mesh=mesh,
        in_specs=placed,
        out_specs=(P("dp", "mp"), P("mp", None, "dp"), P("dp", None)),
        check_vma=False,
    )
```

```python
import functools

import jax
import jax.numpy as jnp
from jax import lax
from jax.experimental import pallas as pl
from jax.experimental.pallas import tpu as pltpu
from jax.sharding import PartitionSpec as P

clip_low = 0.8
clip_high = 1.2
norm_eps = 1e-06
f32 = jnp.float32
bf16 = jnp.bfloat16
lanes = 128


def z_shift(step, nz):
    return [(2 * z + c, 2 * ((z + step) % nz) + c) for z in range(nz) for c in range(2)]


def core_swap(nz):
    return [(2 * z + c, 2 * z + 1 - c) for z in range(nz) for c in range(2)]


def z_ring(block, nz):
    ahead = back = block
    pieces = [(0, 0, block)]
    for step in range(1, nz // 2):
        ahead = lax.ppermute(ahead, "dp", z_shift(1, nz))
        back = lax.ppermute(back, "dp", z_shift(-1, nz))
        pieces += [(nz - step, 0, ahead), (step, 0, back)]
    half = block.shape[0] // 2
    pieces += [
        (nz // 2, 0, lax.ppermute(ahead[:half], "dp", z_shift(1, nz))),
        (nz // 2, half, lax.ppermute(back[half:], "dp", z_shift(-1, nz))),
    ]
    return pieces


def x_shift(step):
    return [(4 * y + x, 4 * y + (x + step) % 4) for y in range(4) for x in range(4)]


def y_shift(step):
    return [(4 * y + x, 4 * ((y + step) % 4) + x) for y in range(4) for x in range(4)]


def x_stage(nz, flip, far):
    pairs = []
    for z in range(nz):
        for core in range(2):
            for y in range(4):
                for high in range(2):
                    for low in range(2):
                        source = (2 * z + core) * 16 + 4 * y + 2 * high + low
                        target = (2 * z + (low ^ flip)) * 16 + 4 * y + 2 * (high ^ far) + core
                        pairs.append((source, target))
    return pairs


def y_stage(step):
    pairs = []
    for group in range(16):
        for y in range(4):
            for x in range(4):
                target = (4 * ((y + step) % 4) + x) * 16 + group
                pairs.append((group * 16 + 4 * y + x, target))
    return pairs


def proj_kernel(acts_ref, down_ref, proj_ref):
    groups, _, slots, wide = acts_ref.shape
    width = down_ref.shape[1]
    acts = acts_ref[:, 0, :, :width].reshape(groups * slots, width)
    out = jnp.dot(acts, down_ref[0], preferred_element_type=f32)
    proj_ref[...] = out.reshape(proj_ref.shape)


def slot_kernel(group_ref, side_ref, rows0, rows1, rows2, rows3, proj_ref, weighted_ref, gate_ref):
    groups, per_expert, slots, _ = side_ref.shape
    tokens, width = rows0.shape[1:]
    count = per_expert * slots
    column = lax.broadcasted_iota(jnp.int32, (count, tokens), 1)
    gates = jnp.zeros((count, lanes), f32)
    for place in range(groups):
        group = group_ref[place]
        rows_ref = (rows0, rows1, rows2, rows3)[place // 4]
        side = side_ref[group].reshape(count, lanes).astype(f32)
        match = jnp.where(column.astype(f32) == side[:, 1:2], 1.0, 0.0).astype(bf16)
        rows = jnp.dot(match, rows_ref[place % 4], preferred_element_type=f32)
        proj = proj_ref[:, group].reshape(count, width)
        gate = jnp.sum(rows * proj, axis=1, keepdims=True)
        gates = jnp.where(column == group, gate, gates)
        weighted = (side[:, 0:1] * rows).astype(bf16)
        weighted_ref[:, group] = weighted.reshape(per_expert, slots, width)
    gate_ref[...] = gates.T[:groups]


def hidden_kernel(nz, place_ref, grad_ref, *refs):
    count = nz + 1
    pieces, out_ref, held, sems = refs[:count], refs[count], refs[count + 1], refs[count + 2]
    z_index, core, x_high, x_low = [place_ref[i] for i in range(4)]
    copies = []
    half = pieces[0].shape[0] // 2
    for number, piece in enumerate(pieces):
        target = held.at[number]
        if number >= nz - 1:
            first = half * (number - nz + 1)
            target = held.at[nz - 1, first : first + half]
        copies.append(pltpu.make_async_copy(piece, target, sems.at[number]))
        copies[-1].start()
    tokens = grad_ref.shape[0] // 2
    grad = grad_ref[...]
    for number in range(nz):
        copies[number].wait()
        if number == nz - 1:
            copies[nz].wait()
        step = (number + 1) // 2
        offset = step if number % 2 == 0 else nz - step
        if number == nz - 1:
            offset = nz // 2
        part = lax.dot_general(
            grad, held[number], (((1,), (1,)), ((), ())), preferred_element_type=f32
        )
        block = lax.rem(z_index + offset, nz)
        far_x = lax.rem(block % 2 + x_high, 2)
        own = lax.rem(core + x_low, 2)
        out_ref[own, far_x, block // 2] = part[:tokens]
        out_ref[1 - own, far_x, block // 2] = part[tokens:]


def down_kernel(acts_ref, weighted_ref, out_ref):
    groups, _, slots, wide = acts_ref.shape
    width = out_ref.shape[1]
    acts = acts_ref[:, 0, :, :width].reshape(groups * slots, width)
    weighted = weighted_ref[0].reshape(groups * slots, weighted_ref.shape[3])
    out_ref[0] = lax.dot_general(
        acts, weighted, (((0,), (0,)), ((), ())), preferred_element_type=f32
    ).astype(bf16)


def local(
    residual,
    norm_gain,
    head_weight,
    token_ids,
    old_logp,
    advantages,
    resp_mask,
    routes,
    combine_weights,
    expert_acts,
    down_weight,
):
    tokens, model_width = residual.shape
    block, vocab_dev = head_weight.shape
    per_expert, _, capacity, hidden_width = expert_acts.shape
    dp_count = lax.axis_size("dp")
    mp_count = lax.axis_size("mp")
    nz = dp_count // 2
    dp_index = lax.axis_index("dp")
    mp_index = lax.axis_index("mp")
    z_index, core = dp_index // 2, dp_index % 2
    y_index, x_index = mp_index // 4, mp_index % 4
    x_high, x_low = x_index // 2, x_index % 2
    both = ("dp", "mp")
    turn = [(p * mp_count + q, q * mp_count + p) for p in range(dp_count) for q in range(mp_count)]
    experts_all = per_expert * mp_count
    swap = functools.partial(lax.ppermute, axis_name="dp", perm=core_swap(nz))

    head_pieces = z_ring(head_weight, nz)

    stream = residual.astype(f32)
    inv_rms = lax.rsqrt(jnp.mean(stream * stream, axis=1, keepdims=True) + norm_eps)
    normed = (stream * inv_rms * norm_gain[None, :]).astype(bf16)
    by_block = normed.reshape(tokens, nz, 2, block).transpose(2, 1, 0, 3)
    mine = lax.dynamic_index_in_dim(by_block, core, 0, keepdims=False)
    theirs = lax.dynamic_index_in_dim(by_block, 1 - core, 0, keepdims=False)
    chip_normed = jnp.concatenate([mine, swap(theirs)], axis=1)

    turned_stream = lax.ppermute(
        lax.dynamic_slice_in_dim(residual, mp_index * block, block, 1), both, turn
    )

    expert_ids = jnp.arange(experts_all, dtype=jnp.int32)
    hit_routes = routes[:, :, None] == expert_ids[None, None, :]
    hit_token = jnp.sum(hit_routes.astype(jnp.int32), axis=1)
    before = jnp.cumsum(hit_token, axis=0) - hit_token
    slot_ids = jnp.arange(capacity, dtype=jnp.int32)
    matches = (hit_token.T[:, None, :] == 1) & (before.T[:, None, :] == slot_ids[None, :, None])
    weight_token = jnp.sum(
        jnp.where(hit_routes, combine_weights[:, :, None].astype(f32), 0.0), axis=1
    )
    first_expert = mp_index * per_expert
    own_matches = lax.dynamic_slice_in_dim(matches, first_expert, per_expert, 0)
    own_weights = lax.dynamic_slice_in_dim(weight_token, first_expert, per_expert, 1)
    slot_weight = jnp.sum(jnp.where(own_matches, own_weights.T[:, None, :], 0.0), axis=2)
    token_numbers = jnp.arange(tokens, dtype=jnp.int32)
    slot_token = jnp.sum(jnp.where(own_matches, token_numbers[None, None, :] + 1, 0), axis=2) - 1
    lane = jnp.arange(lanes, dtype=jnp.int32)
    side = jnp.where(
        lane == 0,
        slot_weight[:, :, None],
        jnp.where(lane == 1, slot_token.astype(f32)[:, :, None], 0.0),
    ).astype(bf16)
    acts_block = jnp.concatenate([expert_acts[:, 0], side], axis=2)

    def features_of(offset, first, piece):
        return lax.dynamic_index_in_dim(
            chip_normed, lax.rem(z_index + offset, nz), 0, keepdims=False
        )[:, first : first + piece.shape[0]]

    partial = jnp.zeros((2 * tokens, vocab_dev), f32)
    for offset, first, piece in head_pieces[:-2]:
        partial = partial + jnp.dot(
            features_of(offset, first, piece), piece, preferred_element_type=f32
        )
    own_part, other_part = partial[:tokens], partial[tokens:]
    for offset, first, piece in head_pieces[-2:]:
        features = features_of(offset, first, piece)
        other_part = other_part + jnp.dot(features[tokens:], piece, preferred_element_type=f32)
        own_part = own_part + jnp.dot(features[:tokens], piece, preferred_element_type=f32)
    logits = own_part + swap(other_part)

    local_ids = token_ids - mp_index * vocab_dev
    column = jnp.arange(vocab_dev, dtype=jnp.int32)
    onehot = column[None, :] == local_ids[:, None]
    local_top = jnp.max(logits, axis=1)
    local_exp = jnp.exp(logits - local_top[:, None])
    local_total = jnp.sum(local_exp, axis=1)
    local_mean = jnp.sum(local_exp * logits, axis=1)
    local_picked = jnp.sum(jnp.where(onehot, logits, 0.0), axis=1)
    stats = jnp.stack([local_top, local_total, local_mean, local_picked])
    stats = lax.all_to_all(
        jnp.broadcast_to(stats[None], (mp_count, 4, tokens)), "mp", 0, 0, tiled=True
    )
    row_top = jnp.max(stats[:, 0], axis=0)
    rescale = jnp.exp(stats[:, 0] - row_top[None])
    row_total = jnp.sum(stats[:, 1] * rescale, axis=0)
    mean_logit = jnp.sum(stats[:, 2] * rescale, axis=0) / row_total
    picked = jnp.sum(stats[:, 3], axis=0)

    logp = picked - row_top - jnp.log(row_total)
    prob_ratio = jnp.exp(logp - old_logp)
    weight_row = -jnp.clip(prob_ratio, clip_low, clip_high) * advantages * resp_mask.astype(f32)
    inner = weight_row * (picked - mean_logit) / model_width
    turned_rows = lax.ppermute(jnp.stack([inv_rms[:, 0], inner]), both, turn)
    logit_grad = (
        weight_row[:, None]
        * (onehot.astype(f32) - jnp.exp(logits - row_top[:, None]) / row_total[:, None])
    ).astype(bf16)
    chip_grad = jnp.concatenate([logit_grad, swap(logit_grad)], axis=0)

    place = jnp.stack([z_index, core, x_high, x_low]).astype(jnp.int32)
    hidden = pl.pallas_call(
        functools.partial(hidden_kernel, nz),
        grid_spec=pltpu.PrefetchScalarGridSpec(
            num_scalar_prefetch=1,
            grid=(1,),
            in_specs=[pl.BlockSpec((2 * tokens, vocab_dev), lambda n, place: (0, 0))]
            + [pl.BlockSpec(memory_space=pl.ANY)] * (nz + 1),
            out_specs=pl.BlockSpec((2, 2, 4, tokens, block), lambda n, place: (0, 0, 0, 0, 0)),
            scratch_shapes=[
                pltpu.VMEM((nz, block, vocab_dev), bf16),
                pltpu.SemaphoreType.DMA((nz + 1,)),
            ],
        ),
        out_shape=jax.ShapeDtypeStruct((2, 2, 4, tokens, block), f32),
        compiler_params=pltpu.CompilerParams(vmem_limit_bytes=40 * 1024 * 1024),
    )(place, chip_grad, *[piece for _, _, piece in head_pieces])

    rows_sum = None
    for flip in range(2):
        for far in range(2):
            moved = lax.ppermute(hidden[flip, far], both, x_stage(nz, flip, far))
            rows_sum = moved if rows_sum is None else rows_sum + moved
    hidden_grad = None
    for step in range(4):
        sent = lax.dynamic_index_in_dim(rows_sum, lax.rem(y_index + step, 4), 0, keepdims=False)
        moved = lax.ppermute(sent, both, y_stage(step))
        hidden_grad = moved if hidden_grad is None else hidden_grad + moved

    my_gain = lax.dynamic_slice_in_dim(norm_gain, dp_index * block, block, 0)
    turned_rms, turned_inner = turned_rows[0][:, None], turned_rows[1][:, None]
    scaled_grad = my_gain[None, :] * hidden_grad
    turned_resid = turned_rms * (
        scaled_grad - turned_stream.astype(f32) * turned_rms * turned_inner
    )
    stream_grad = turned_resid.astype(bf16)
    resid_grad = lax.ppermute(turned_resid, both, turn)

    in_row = [stream_grad] + [lax.ppermute(stream_grad, "mp", x_shift(k)) for k in (1, 2, 3)]
    in_row = jnp.stack(in_row)
    all_rows = [in_row] + [lax.ppermute(in_row, "mp", y_shift(k)) for k in (1, 2, 3)]
    steps = jnp.arange(16, dtype=jnp.int32)
    group_of = 4 * lax.rem(y_index + 4 - steps // 4, 4) + lax.rem(x_index + 4 - steps % 4, 4)

    acts_block, _ = lax.optimization_barrier((acts_block, (head_pieces[-1][2], head_pieces[-2][2])))
    acts_all = lax.all_gather(acts_block, "dp", axis=0, tiled=False)

    wide = hidden_width + lanes
    proj = pl.pallas_call(
        proj_kernel,
        grid=(per_expert,),
        in_specs=[
            pl.BlockSpec((dp_count, 1, capacity, wide), lambda e: (0, e, 0, 0)),
            pl.BlockSpec((1, hidden_width, block), lambda e: (e, 0, 0)),
        ],
        out_specs=pl.BlockSpec((1, dp_count, capacity, block), lambda e: (e, 0, 0, 0)),
        out_shape=jax.ShapeDtypeStruct((per_expert, dp_count, capacity, block), f32),
        compiler_params=pltpu.CompilerParams(vmem_limit_bytes=32 * 1024 * 1024),
    )(acts_all, down_weight)
    weighted, gate = pl.pallas_call(
        slot_kernel,
        grid_spec=pltpu.PrefetchScalarGridSpec(
            num_scalar_prefetch=1,
            grid=(1,),
            in_specs=[
                pl.BlockSpec(
                    (dp_count, per_expert, capacity, lanes),
                    lambda n, group: (0, 0, 0, hidden_width // lanes),
                ),
            ]
            + [pl.BlockSpec((4, tokens, block), lambda n, group: (0, 0, 0))] * 4
            + [pl.BlockSpec((per_expert, dp_count, capacity, block), lambda n, group: (0, 0, 0, 0))],
            out_specs=[
                pl.BlockSpec((per_expert, dp_count, capacity, block), lambda n, group: (0, 0, 0, 0)),
                pl.BlockSpec((dp_count, per_expert * capacity), lambda n, group: (0, 0)),
            ],
        ),
        out_shape=[
            jax.ShapeDtypeStruct((per_expert, dp_count, capacity, block), bf16),
            jax.ShapeDtypeStruct((dp_count, per_expert * capacity), f32),
        ],
        compiler_params=pltpu.CompilerParams(vmem_limit_bytes=32 * 1024 * 1024),
    )(group_of.astype(jnp.int32), acts_all, *all_rows, proj)
    down_grad = pl.pallas_call(
        down_kernel,
        grid=(per_expert,),
        in_specs=[
            pl.BlockSpec((dp_count, 1, capacity, wide), lambda e: (0, e, 0, 0)),
            pl.BlockSpec((1, dp_count, capacity, block), lambda e: (e, 0, 0, 0)),
        ],
        out_specs=pl.BlockSpec((1, hidden_width, block), lambda e: (e, 0, 0)),
        out_shape=jax.ShapeDtypeStruct((per_expert, hidden_width, block), bf16),
        compiler_params=pltpu.CompilerParams(vmem_limit_bytes=32 * 1024 * 1024),
    )(acts_all, weighted)

    group_gate = jnp.sum(
        lax.all_to_all(gate[:, None, :], "dp", 0, 0, tiled=True), axis=0, keepdims=True
    )
    slot_gate = lax.all_to_all(
        jnp.broadcast_to(group_gate, (mp_count, 1, per_expert * capacity)), "mp", 0, 0, tiled=True
    ).reshape(experts_all, capacity)
    per_token = jnp.sum(jnp.where(matches, slot_gate[:, :, None], 0.0), axis=1)
    gate_grad = jnp.sum(jnp.where(hit_routes, per_token.T[:, None, :], 0.0), axis=2)
    return (resid_grad, down_grad, gate_grad)


def solution(mesh):
    placed = (
        P("dp", None),
        P(),
        P("dp", "mp"),
        P("dp"),
        P("dp"),
        P("dp"),
        P("dp"),
        P("dp", None),
        P("dp", None),
        P("mp", "dp", None, None),
        P("mp", None, "dp"),
    )
    return jax.shard_map(
        local,
        mesh=mesh,
        in_specs=placed,
        out_specs=(P("dp", "mp"), P("mp", None, "dp"), P("dp", None)),
        check_vma=False,
    )
```

```python
import functools

import jax
import jax.numpy as jnp
from jax import lax
from jax.experimental import pallas as pl
from jax.experimental.pallas import tpu as pltpu
from jax.sharding import PartitionSpec as P

clip_low = 0.8
clip_high = 1.2
norm_eps = 1e-06
f32 = jnp.float32
bf16 = jnp.bfloat16
lanes = 128


def z_shift(step, nz):
    return [(2 * z + c, 2 * ((z + step) % nz) + c) for z in range(nz) for c in range(2)]


def core_swap(nz):
    return [(2 * z + c, 2 * z + 1 - c) for z in range(nz) for c in range(2)]


def sum_turn(nz):
    return [
        ((2 * z + c) * 16 + 2 * b + low, (2 * b + c) * 16 + 2 * z + low)
        for z in range(nz) for c in range(2) for b in range(nz) for low in range(2)
    ]


def proj_kernel(acts_ref, down_ref, proj_ref):
    groups, _, slots, wide = acts_ref.shape
    acts = acts_ref[:, 0].reshape(groups * slots, wide)
    out = jnp.dot(acts, down_ref[0], preferred_element_type=f32)
    proj_ref[...] = out.reshape(proj_ref.shape)


def gate_kernel(slot_token_ref, rows_ref, proj_ref, gate_ref):
    shards, count, width = proj_ref.shape
    tokens = rows_ref.shape[0]
    column = lax.broadcasted_iota(jnp.int32, (count, tokens), 1)
    slot_token = slot_token_ref[...]
    stream_rows = rows_ref[...]
    gates = jnp.zeros((count, lanes), f32)
    for shard in range(shards):
        match = jnp.where(column == slot_token[:, shard : shard + 1], 1.0, 0.0).astype(bf16)
        rows = jnp.dot(match, stream_rows, preferred_element_type=f32)
        gate = jnp.sum(rows * proj_ref[shard], axis=1, keepdims=True)
        gates = jnp.where(column == shard, gate, gates)
    gate_ref[...] = gates.T[:shards]


def hidden_kernel(nz, place_ref, grad_ref, *refs):
    count = nz + 1
    pieces, out_ref, held, sems = refs[:count], refs[count], refs[count + 1], refs[count + 2]
    z_index, core = place_ref[0], place_ref[1]
    copies = []
    half = pieces[0].shape[0] // 2
    for number, piece in enumerate(pieces):
        target = held.at[number]
        if number >= nz - 1:
            first = half * (number - nz + 1)
            target = held.at[nz - 1, first : first + half]
        copies.append(pltpu.make_async_copy(piece, target, sems.at[number]))
        copies[-1].start()
    tokens = grad_ref.shape[0] // 2
    grad = grad_ref[...]
    for number in range(nz):
        copies[number].wait()
        if number == nz - 1:
            copies[nz].wait()
        step = (number + 1) // 2
        offset = step if number % 2 == 0 else nz - step
        if number == nz - 1:
            offset = nz // 2
        part = lax.dot_general(
            grad, held[number], (((1,), (1,)), ((), ())), preferred_element_type=f32
        )
        block = lax.rem(z_index + offset, nz)
        out_ref[2 * block + core] = part[:tokens]
        out_ref[2 * block + 1 - core] = part[tokens:]


def down_kernel(side_ref, rows_ref, acts_ref, out_ref, weighted):
    groups, per_expert, slots, _ = side_ref.shape
    tokens, width = rows_ref.shape[1:]
    count = per_expert * slots
    expert = pl.program_id(0)

    @pl.when(expert == 0)
    def _():
        column = lax.broadcasted_iota(jnp.int32, (count, tokens), 1).astype(f32)
        for group in range(groups):
            side = side_ref[group].reshape(count, lanes).astype(f32)
            match = jnp.where(column == side[:, 1:2], 1.0, 0.0).astype(bf16)
            rows = jnp.dot(match, rows_ref[group], preferred_element_type=f32)
            made = (side[:, 0:1] * rows).astype(bf16)
            weighted[:, group] = made.reshape(per_expert, slots, width)

    acts = acts_ref[:, 0].reshape(groups * slots, acts_ref.shape[3])
    out_ref[0] = lax.dot_general(
        acts,
        weighted[expert].reshape(groups * slots, width),
        (((0,), (0,)), ((), ())),
        preferred_element_type=f32,
    ).astype(bf16)


def local(
    residual,
    norm_gain,
    head_weight,
    token_ids,
    old_logp,
    advantages,
    resp_mask,
    routes,
    combine_weights,
    expert_acts,
    down_weight,
):
    tokens, model_width = residual.shape
    block, vocab_dev = head_weight.shape
    per_expert, _, capacity, hidden_width = expert_acts.shape
    dp_count = lax.axis_size("dp")
    mp_count = lax.axis_size("mp")
    nz = dp_count // 2
    dp_index = lax.axis_index("dp")
    mp_index = lax.axis_index("mp")
    z_index, core = dp_index // 2, dp_index % 2
    both = ("dp", "mp")
    turn = [(p * mp_count + q, q * mp_count + p) for p in range(dp_count) for q in range(mp_count)]
    experts_all = per_expert * mp_count
    swap = functools.partial(lax.ppermute, axis_name="dp", perm=core_swap(nz))

    stream = residual.astype(f32)
    inv_rms = lax.rsqrt(jnp.mean(stream * stream, axis=1, keepdims=True) + norm_eps)
    normed = (stream * inv_rms * norm_gain[None, :]).astype(bf16)
    by_block = normed.reshape(tokens, nz, 2, block).transpose(2, 1, 0, 3)
    mine = lax.dynamic_index_in_dim(by_block, core, 0, keepdims=False)
    theirs = lax.dynamic_index_in_dim(by_block, 1 - core, 0, keepdims=False)
    chip_normed = jnp.concatenate([mine, swap(theirs)], axis=1)

    turned_stream = lax.ppermute(
        lax.dynamic_slice_in_dim(residual, mp_index * block, block, 1), both, turn
    )

    expert_ids = jnp.arange(experts_all, dtype=jnp.int32)
    hit_routes = routes[:, :, None] == expert_ids[None, None, :]
    hit_token = jnp.sum(hit_routes.astype(jnp.int32), axis=1)
    before = jnp.cumsum(hit_token, axis=0) - hit_token
    slot_ids = jnp.arange(capacity, dtype=jnp.int32)
    matches = (hit_token.T[:, None, :] == 1) & (before.T[:, None, :] == slot_ids[None, :, None])
    weight_token = jnp.sum(
        jnp.where(hit_routes, combine_weights[:, :, None].astype(f32), 0.0), axis=1
    )
    first_expert = mp_index * per_expert
    token_numbers = jnp.arange(tokens, dtype=jnp.int32)
    slot_token = jnp.sum(jnp.where(matches, token_numbers[None, None, :] + 1, 0), axis=2) - 1
    own_matches = lax.dynamic_slice_in_dim(matches, first_expert, per_expert, 0)
    own_weights = lax.dynamic_slice_in_dim(weight_token, first_expert, per_expert, 1)
    own_slot_token = lax.dynamic_slice_in_dim(slot_token, first_expert, per_expert, 0)
    slot_weight = jnp.sum(jnp.where(own_matches, own_weights.T[:, None, :], 0.0), axis=2)
    turned_slots = lax.ppermute(
        slot_token.reshape(mp_count, per_expert * capacity).T, both, turn
    )
    lane = jnp.arange(lanes, dtype=jnp.int32)
    side = jnp.where(
        lane == 0,
        slot_weight[:, :, None],
        jnp.where(lane == 1, own_slot_token.astype(f32)[:, :, None], 0.0),
    ).astype(bf16)
    acts_block = jnp.concatenate([expert_acts[:, 0], side], axis=2)

    acts_all = lax.all_gather(acts_block, "dp", axis=0, tiled=False)
    proj = pl.pallas_call(
        proj_kernel,
        grid=(per_expert,),
        in_specs=[
            pl.BlockSpec((dp_count, 1, capacity, hidden_width), lambda e: (0, e, 0, 0)),
            pl.BlockSpec((1, hidden_width, block), lambda e: (e, 0, 0)),
        ],
        out_specs=pl.BlockSpec((dp_count, 1, capacity, block), lambda e: (0, e, 0, 0)),
        out_shape=jax.ShapeDtypeStruct((dp_count, per_expert, capacity, block), f32),
        compiler_params=pltpu.CompilerParams(vmem_limit_bytes=32 * 1024 * 1024),
    )(acts_all, down_weight)

    def logits_of(rows, offset, first, piece):
        features = lax.dynamic_index_in_dim(
            chip_normed, lax.rem(z_index + offset, nz), 0, keepdims=False
        )[rows, first : first + piece.shape[0]]
        return jnp.dot(features, piece, preferred_element_type=f32)

    everything = slice(0, 2 * tokens)
    ahead = back = head_weight
    head_pieces = [(0, 0, head_weight)]
    partial = None
    for step in range(1, nz // 2):
        if step == 2:
            ahead, back, chip_normed = lax.optimization_barrier((ahead, back, chip_normed))
        if step > 2:
            ahead, back, partial = lax.optimization_barrier((ahead, back, partial))
        if step >= 2:
            done = head_pieces[-2:] if step > 2 else head_pieces
            for offset, first, piece in done:
                added = logits_of(everything, offset, first, piece)
                partial = added if partial is None else partial + added
        ahead = lax.ppermute(ahead, "dp", z_shift(1, nz))
        back = lax.ppermute(back, "dp", z_shift(-1, nz))
        head_pieces += [(nz - step, 0, ahead), (step, 0, back)]
    ahead, back, partial, proj = lax.optimization_barrier((ahead, back, partial, proj))
    half = block // 2
    last_pieces = [
        (nz // 2, 0, lax.ppermute(ahead[:half], "dp", z_shift(1, nz))),
        (nz // 2, half, lax.ppermute(back[half:], "dp", z_shift(-1, nz))),
    ]
    turned_proj = lax.all_to_all(
        proj.reshape(dp_count, per_expert * capacity, block), "mp", 0, 0, tiled=True
    )
    for offset, first, piece in head_pieces[-2:]:
        partial = partial + logits_of(everything, offset, first, piece)
    own_part, other_part = partial[:tokens], partial[tokens:]
    for offset, first, piece in last_pieces:
        other_part = other_part + logits_of(slice(tokens, None), offset, first, piece)
        own_part = own_part + logits_of(slice(0, tokens), offset, first, piece)
    head_pieces += last_pieces
    logits = own_part + swap(other_part)

    local_ids = token_ids - mp_index * vocab_dev
    column = jnp.arange(vocab_dev, dtype=jnp.int32)
    onehot = column[None, :] == local_ids[:, None]
    local_top = jnp.max(logits, axis=1)
    local_exp = jnp.exp(logits - local_top[:, None])
    local_total = jnp.sum(local_exp, axis=1)
    local_mean = jnp.sum(local_exp * logits, axis=1)
    local_picked = jnp.sum(jnp.where(onehot, logits, 0.0), axis=1)
    stats = jnp.stack([local_top, local_total, local_mean, local_picked])
    stats = lax.all_to_all(
        jnp.broadcast_to(stats[None], (mp_count, 4, tokens)), "mp", 0, 0, tiled=True
    )
    row_top = jnp.max(stats[:, 0], axis=0)
    rescale = jnp.exp(stats[:, 0] - row_top[None])
    row_total = jnp.sum(stats[:, 1] * rescale, axis=0)
    mean_logit = jnp.sum(stats[:, 2] * rescale, axis=0) / row_total
    picked = jnp.sum(stats[:, 3], axis=0)

    logp = picked - row_top - jnp.log(row_total)
    prob_ratio = jnp.exp(logp - old_logp)
    weight_row = -jnp.clip(prob_ratio, clip_low, clip_high) * advantages * resp_mask.astype(f32)
    inner = weight_row * (picked - mean_logit) / model_width
    turned_rows = lax.ppermute(jnp.stack([inv_rms[:, 0], inner]), both, turn)
    logit_grad = (
        weight_row[:, None]
        * (onehot.astype(f32) - jnp.exp(logits - row_top[:, None]) / row_total[:, None])
    ).astype(bf16)
    chip_grad = jnp.concatenate([logit_grad, swap(logit_grad)], axis=0)

    place = jnp.stack([z_index, core]).astype(jnp.int32)
    hidden = pl.pallas_call(
        functools.partial(hidden_kernel, nz),
        grid_spec=pltpu.PrefetchScalarGridSpec(
            num_scalar_prefetch=1,
            grid=(1,),
            in_specs=[pl.BlockSpec((2 * tokens, vocab_dev), lambda n, place: (0, 0))]
            + [pl.BlockSpec(memory_space=pl.ANY)] * (nz + 1),
            out_specs=pl.BlockSpec((mp_count, tokens, block), lambda n, place: (0, 0, 0)),
            scratch_shapes=[
                pltpu.VMEM((nz, block, vocab_dev), bf16),
                pltpu.SemaphoreType.DMA((nz + 1,)),
            ],
        ),
        out_shape=jax.ShapeDtypeStruct((mp_count, tokens, block), f32),
        compiler_params=pltpu.CompilerParams(vmem_limit_bytes=40 * 1024 * 1024),
    )(place, chip_grad, *[piece for _, _, piece in head_pieces])

    hidden, turned_proj = lax.optimization_barrier((hidden, turned_proj))
    hidden_grad = jnp.sum(lax.all_to_all(hidden, "mp", 0, 0, tiled=True), axis=0)
    hidden_grad = lax.ppermute(hidden_grad, both, sum_turn(nz))

    my_gain = lax.dynamic_slice_in_dim(norm_gain, dp_index * block, block, 0)
    turned_rms, turned_inner = turned_rows[0][:, None], turned_rows[1][:, None]
    scaled_grad = my_gain[None, :] * hidden_grad
    turned_resid = turned_rms * (
        scaled_grad - turned_stream.astype(f32) * turned_rms * turned_inner
    )
    stream_grad = turned_resid.astype(bf16)
    resid_grad = lax.ppermute(turned_resid, both, turn)

    all_rows = lax.all_to_all(
        jnp.broadcast_to(stream_grad[None], (mp_count, tokens, block)), "mp", 0, 0, tiled=True
    )
    gate = pl.pallas_call(
        gate_kernel,
        out_shape=jax.ShapeDtypeStruct((mp_count, per_expert * capacity), f32),
        compiler_params=pltpu.CompilerParams(vmem_limit_bytes=32 * 1024 * 1024),
    )(turned_slots, stream_grad, turned_proj)
    down_grad = pl.pallas_call(
        down_kernel,
        grid=(per_expert,),
        in_specs=[
            pl.BlockSpec(
                (dp_count, per_expert, capacity, lanes), lambda e: (0, 0, 0, hidden_width // lanes)
            ),
            pl.BlockSpec((dp_count, tokens, block), lambda e: (0, 0, 0)),
            pl.BlockSpec((dp_count, 1, capacity, hidden_width), lambda e: (0, e, 0, 0)),
        ],
        out_specs=pl.BlockSpec((1, hidden_width, block), lambda e: (e, 0, 0)),
        out_shape=jax.ShapeDtypeStruct((per_expert, hidden_width, block), bf16),
        scratch_shapes=[pltpu.VMEM((per_expert, dp_count, capacity, block), bf16)],
        compiler_params=pltpu.CompilerParams(vmem_limit_bytes=40 * 1024 * 1024),
    )(acts_all, all_rows, acts_all)

    gate = lax.ppermute(gate, both, turn)
    slot_gate = jnp.sum(
        lax.all_to_all(
            jnp.broadcast_to(gate[None], (mp_count,) + gate.shape), "mp", 0, 0, tiled=True
        ),
        axis=0,
    ).reshape(experts_all, capacity)
    per_token = jnp.sum(jnp.where(matches, slot_gate[:, :, None], 0.0), axis=1)
    gate_grad = jnp.sum(jnp.where(hit_routes, per_token.T[:, None, :], 0.0), axis=2)
    return (resid_grad, down_grad, gate_grad)


def solution(mesh):
    placed = (
        P("dp", None),
        P(),
        P("dp", "mp"),
        P("dp"),
        P("dp"),
        P("dp"),
        P("dp"),
        P("dp", None),
        P("dp", None),
        P("mp", "dp", None, None),
        P("mp", None, "dp"),
    )
    return jax.shard_map(
        local,
        mesh=mesh,
        in_specs=placed,
        out_specs=(P("dp", "mp"), P("mp", None, "dp"), P("dp", None)),
        check_vma=False,
    )
```

```python
import functools

import jax
import jax.numpy as jnp
from jax import lax
from jax.experimental import pallas as pl
from jax.experimental.pallas import tpu as pltpu
from jax.sharding import PartitionSpec as P

clip_low = 0.8
clip_high = 1.2
norm_eps = 1e-06
f32 = jnp.float32
bf16 = jnp.bfloat16
lanes = 128


def z_shift(step, nz):
    return [(2 * z + c, 2 * ((z + step) % nz) + c) for z in range(nz) for c in range(2)]


def core_swap(nz):
    return [(2 * z + c, 2 * z + 1 - c) for z in range(nz) for c in range(2)]


def sum_turn(nz):
    return [
        ((2 * z + c) * 16 + 2 * b + low, (2 * b + c) * 16 + 2 * z + low)
        for z in range(nz) for c in range(2) for b in range(nz) for low in range(2)
    ]


def acts_of(refs, expert, wide):
    parts = []
    for core in range(2):
        mine = refs[core * len(refs) // 2 : (core + 1) * len(refs) // 2]
        parts += [ref[0, :, :wide] for ref in mine[:-2]]
        first = mine[-2][0, :, :wide]
        parts.append(jnp.where(expert < 2, first, mine[-1][0, :, :wide]))
    return jnp.concatenate(parts, axis=0)


def proj_kernel(group_ref, down_ref, *refs):
    acts_refs, proj_ref = refs[:-1], refs[-1]
    acts = acts_of(acts_refs, pl.program_id(0), down_ref.shape[1])
    out = jnp.dot(acts, down_ref[0], preferred_element_type=f32)
    slots = proj_ref.shape[2]
    for place in range(proj_ref.shape[0]):
        proj_ref[group_ref[place], 0] = out[place * slots : (place + 1) * slots]


def gate_kernel(slot_token_ref, rows_ref, proj_ref, gate_ref):
    shards, count, width = proj_ref.shape
    tokens = rows_ref.shape[0]
    column = lax.broadcasted_iota(jnp.int32, (count, tokens), 1)
    slot_token = slot_token_ref[...]
    stream_rows = rows_ref[...]
    gates = jnp.zeros((count, lanes), f32)
    for shard in range(shards):
        match = jnp.where(column == slot_token[:, shard : shard + 1], 1.0, 0.0).astype(bf16)
        rows = jnp.dot(match, stream_rows, preferred_element_type=f32)
        gate = jnp.sum(rows * proj_ref[shard], axis=1, keepdims=True)
        gates = jnp.where(column == shard, gate, gates)
    gate_ref[...] = gates.T[:shards]


def hidden_kernel(nz, place_ref, grad_ref, *refs):
    pieces, out_ref = refs[: nz + 1], refs[nz + 1]
    z_index, core = place_ref[0], place_ref[1]
    tokens = grad_ref.shape[0] // 2
    half = pieces[0].shape[0] // 2
    grad = grad_ref[...]
    for number in range(nz + 1):
        step = (number + 1) // 2
        offset = step if number % 2 == 0 else nz - step
        first = 0
        if number >= nz - 1:
            offset, first = nz // 2, half * (number - nz + 1)
        part = lax.dot_general(
            pieces[number][...], grad, (((1,), (1,)), ((), ())), preferred_element_type=f32
        ).astype(out_ref.dtype)
        rows = slice(first, first + part.shape[0])
        block = lax.rem(z_index + offset, nz)
        out_ref[2 * block + core, rows] = part[:, :tokens]
        out_ref[2 * block + 1 - core, rows] = part[:, tokens:]


def down_kernel(group_ref, rows_ref, *refs):
    count = (len(refs) - 2) // 2
    side_refs, acts_refs, out_ref, weighted = refs[:count], refs[count:-2], refs[-2], refs[-1]
    per_expert, places, slots, _ = weighted.shape
    sides = []
    for core in range(2):
        mine = side_refs[core * count // 2 : (core + 1) * count // 2]
        sides += [(ref,) for ref in mine[:-2]] + [mine[-2:]]
    tokens, width = rows_ref.shape[1:]
    rows_out = per_expert * slots
    expert = pl.program_id(0)

    @pl.when(expert == 0)
    def _():
        column = lax.broadcasted_iota(jnp.int32, (rows_out, tokens), 1).astype(f32)
        for place in range(places):
            side = jnp.concatenate([ref[...] for ref in sides[place]], axis=0)
            side = side.reshape(rows_out, lanes).astype(f32)
            match = jnp.where(column == side[:, 1:2], 1.0, 0.0).astype(bf16)
            rows = jnp.dot(match, rows_ref[group_ref[place]], preferred_element_type=f32)
            made = (side[:, 0:1] * rows).astype(bf16)
            weighted[:, place] = made.reshape(per_expert, slots, width)

    acts = acts_of(acts_refs, expert, out_ref.shape[1])
    out_ref[0] = lax.dot_general(
        acts,
        weighted[expert].reshape(places * slots, width),
        (((0,), (0,)), ((), ())),
        preferred_element_type=f32,
    ).astype(bf16)


def local(
    residual,
    norm_gain,
    head_weight,
    token_ids,
    old_logp,
    advantages,
    resp_mask,
    routes,
    combine_weights,
    expert_acts,
    down_weight,
):
    tokens, model_width = residual.shape
    block, vocab_dev = head_weight.shape
    per_expert, _, capacity, hidden_width = expert_acts.shape
    dp_count = lax.axis_size("dp")
    mp_count = lax.axis_size("mp")
    nz = dp_count // 2
    dp_index = lax.axis_index("dp")
    mp_index = lax.axis_index("mp")
    z_index, core = dp_index // 2, dp_index % 2
    both = ("dp", "mp")
    turn = [(p * mp_count + q, q * mp_count + p) for p in range(dp_count) for q in range(mp_count)]
    experts_all = per_expert * mp_count
    swap = functools.partial(lax.ppermute, axis_name="dp", perm=core_swap(nz))

    stream = residual.astype(f32)
    inv_rms = lax.rsqrt(jnp.mean(stream * stream, axis=1, keepdims=True) + norm_eps)
    normed = (stream * inv_rms * norm_gain[None, :]).astype(bf16)
    by_block = normed.reshape(tokens, nz, 2, block).transpose(2, 1, 0, 3)
    mine = lax.dynamic_index_in_dim(by_block, core, 0, keepdims=False)
    theirs = lax.dynamic_index_in_dim(by_block, 1 - core, 0, keepdims=False)
    chip_normed = jnp.concatenate([mine, swap(theirs)], axis=1)

    turned_stream = lax.ppermute(
        lax.dynamic_slice_in_dim(residual, mp_index * block, block, 1), both, turn
    )

    expert_ids = jnp.arange(experts_all, dtype=jnp.int32)
    hit_routes = routes[:, :, None] == expert_ids[None, None, :]
    hit_token = jnp.sum(hit_routes.astype(jnp.int32), axis=1)
    before = jnp.cumsum(hit_token, axis=0) - hit_token
    slot_ids = jnp.arange(capacity, dtype=jnp.int32)
    matches = (hit_token.T[:, None, :] == 1) & (before.T[:, None, :] == slot_ids[None, :, None])
    weight_token = jnp.sum(
        jnp.where(hit_routes, combine_weights[:, :, None].astype(f32), 0.0), axis=1
    )
    first_expert = mp_index * per_expert
    token_numbers = jnp.arange(tokens, dtype=jnp.int32)
    slot_token = jnp.sum(jnp.where(matches, token_numbers[None, None, :] + 1, 0), axis=2) - 1
    own_matches = lax.dynamic_slice_in_dim(matches, first_expert, per_expert, 0)
    own_weights = lax.dynamic_slice_in_dim(weight_token, first_expert, per_expert, 1)
    own_slot_token = lax.dynamic_slice_in_dim(slot_token, first_expert, per_expert, 0)
    slot_weight = jnp.sum(jnp.where(own_matches, own_weights.T[:, None, :], 0.0), axis=2)
    turned_slots = lax.ppermute(
        slot_token.reshape(mp_count, per_expert * capacity).T, both, turn
    )
    lane = jnp.arange(lanes, dtype=jnp.int32)
    side = jnp.where(
        lane == 0,
        slot_weight[:, :, None],
        jnp.where(lane == 1, own_slot_token.astype(f32)[:, :, None], 0.0),
    ).astype(bf16)
    acts_block = jnp.concatenate([expert_acts[:, 0], side], axis=2)

    def logits_of(rows, offset, first, piece):
        features = lax.dynamic_index_in_dim(
            chip_normed, lax.rem(z_index + offset, nz), 0, keepdims=False
        )[rows, first : first + piece.shape[0]]
        return jnp.dot(features, piece, preferred_element_type=f32)

    everything = slice(0, 2 * tokens)
    ahead = lax.ppermute(head_weight, "dp", z_shift(1, nz))
    back = lax.ppermute(head_weight, "dp", z_shift(-1, nz))
    head_pieces = [(0, 0, head_weight), (nz - 1, 0, ahead), (1, 0, back)]

    acts_ahead = acts_back = acts_block
    acts_pieces = [acts_block]
    for step in range(1, nz // 2):
        acts_ahead = lax.ppermute(acts_ahead, "dp", z_shift(1, nz))
        acts_back = lax.ppermute(acts_back, "dp", z_shift(-1, nz))
        acts_pieces += [acts_ahead, acts_back]
    ahead, back, chip_normed, acts_ahead, acts_back = lax.optimization_barrier(
        (ahead, back, chip_normed, acts_ahead, acts_back)
    )
    ahead = lax.ppermute(ahead, "dp", z_shift(1, nz))
    back = lax.ppermute(back, "dp", z_shift(-1, nz))
    acts_half = per_expert // 2
    acts_pieces += [
        lax.ppermute(acts_ahead[:acts_half], "dp", z_shift(1, nz)),
        lax.ppermute(acts_back[acts_half:], "dp", z_shift(-1, nz)),
    ]
    acts_pieces += [swap(piece) for piece in acts_pieces]
    partial = logits_of(everything, *head_pieces[0])
    for piece in head_pieces[1:]:
        partial = partial + logits_of(everything, *piece)
    head_pieces += [(nz - 2, 0, ahead), (2, 0, back)]

    offsets = [0]
    for step in range(1, nz // 2):
        offsets += [nz - step, step]
    z_of = lax.rem(z_index + jnp.array(offsets + [nz // 2], jnp.int32), nz)
    group_of = jnp.concatenate([2 * z_of + core, 2 * z_of + 1 - core]).astype(jnp.int32)

    def acts_spec(at):
        at = at % (nz + 1)
        if at < nz - 1:
            return pl.BlockSpec((1, capacity, hidden_width), lambda e, group: (e, 0, 0))
        if at == nz - 1:
            return pl.BlockSpec(
                (1, capacity, hidden_width), lambda e, group: (jnp.minimum(e, acts_half - 1), 0, 0)
            )
        return pl.BlockSpec(
            (1, capacity, hidden_width), lambda e, group: (jnp.maximum(e - acts_half, 0), 0, 0)
        )

    acts_specs = [acts_spec(at) for at in range(2 * nz + 2)]
    proj = pl.pallas_call(
        proj_kernel,
        grid_spec=pltpu.PrefetchScalarGridSpec(
            num_scalar_prefetch=1,
            grid=(per_expert,),
            in_specs=[pl.BlockSpec((1, hidden_width, block), lambda e, group: (e, 0, 0))]
            + acts_specs,
            out_specs=pl.BlockSpec((dp_count, 1, capacity, block), lambda e, group: (0, e, 0, 0)),
        ),
        out_shape=jax.ShapeDtypeStruct((dp_count, per_expert, capacity, block), f32),
        compiler_params=pltpu.CompilerParams(vmem_limit_bytes=58 * 1024 * 1024),
    )(group_of, down_weight, *acts_pieces)
    for step in range(3, nz // 2):
        ahead, back, partial, proj = lax.optimization_barrier((ahead, back, partial, proj))
        ahead = lax.ppermute(ahead, "dp", z_shift(1, nz))
        back = lax.ppermute(back, "dp", z_shift(-1, nz))
        for piece in head_pieces[-2:]:
            partial = partial + logits_of(everything, *piece)
        head_pieces += [(nz - step, 0, ahead), (step, 0, back)]
    turned_proj = lax.all_to_all(
        proj.reshape(dp_count, per_expert * capacity, block), "mp", 0, 0, tiled=True
    )

    ahead, back, partial = lax.optimization_barrier((ahead, back, partial))
    half = block // 2
    last_pieces = [
        (nz // 2, 0, lax.ppermute(ahead[:half], "dp", z_shift(1, nz))),
        (nz // 2, half, lax.ppermute(back[half:], "dp", z_shift(-1, nz))),
    ]
    for piece in head_pieces[-2:]:
        partial = partial + logits_of(everything, *piece)
    own_part, other_part = partial[:tokens], partial[tokens:]
    for piece in last_pieces:
        other_part = other_part + logits_of(slice(tokens, None), *piece)
        own_part = own_part + logits_of(slice(0, tokens), *piece)
    head_pieces += last_pieces
    logits = own_part + swap(other_part)

    local_ids = token_ids - mp_index * vocab_dev
    column = jnp.arange(vocab_dev, dtype=jnp.int32)
    onehot = column[None, :] == local_ids[:, None]
    local_top = jnp.max(logits, axis=1)
    local_exp = jnp.exp(logits - local_top[:, None])
    local_total = jnp.sum(local_exp, axis=1)
    local_mean = jnp.sum(local_exp * logits, axis=1)
    local_picked = jnp.sum(jnp.where(onehot, logits, 0.0), axis=1)
    stats = jnp.stack([local_top, local_total, local_mean, local_picked])
    stats, turned_proj = lax.optimization_barrier((stats, turned_proj))
    stats = lax.all_to_all(
        jnp.broadcast_to(stats[None], (mp_count, 4, tokens)), "mp", 0, 0, tiled=True
    )
    row_top = jnp.max(stats[:, 0], axis=0)
    rescale = jnp.exp(stats[:, 0] - row_top[None])
    row_total = jnp.sum(stats[:, 1] * rescale, axis=0)
    mean_logit = jnp.sum(stats[:, 2] * rescale, axis=0) / row_total
    picked = jnp.sum(stats[:, 3], axis=0)

    logp = picked - row_top - jnp.log(row_total)
    prob_ratio = jnp.exp(logp - old_logp)
    weight_row = -jnp.clip(prob_ratio, clip_low, clip_high) * advantages * resp_mask.astype(f32)
    inner = weight_row * (picked - mean_logit) / model_width
    turned_rows = lax.ppermute(jnp.stack([inv_rms[:, 0], inner]), both, turn)
    logit_grad = (
        weight_row[:, None]
        * (onehot.astype(f32) - jnp.exp(logits - row_top[:, None]) / row_total[:, None])
    ).astype(bf16)
    chip_grad = jnp.concatenate([logit_grad, swap(logit_grad)], axis=0)

    place = jnp.stack([z_index, core]).astype(jnp.int32)
    hidden = pl.pallas_call(
        functools.partial(hidden_kernel, nz),
        in_specs=[pl.BlockSpec(memory_space=pltpu.SMEM)]
        + [pl.BlockSpec(memory_space=pltpu.VMEM)] * (nz + 2),
        out_specs=pl.BlockSpec(memory_space=pltpu.VMEM),
        out_shape=jax.ShapeDtypeStruct((mp_count, block, tokens), bf16),
        compiler_params=pltpu.CompilerParams(vmem_limit_bytes=40 * 1024 * 1024),
    )(place, chip_grad, *[piece for _, _, piece in head_pieces])

    hidden_grad = jnp.sum(
        lax.all_to_all(hidden, "mp", 0, 0, tiled=True).astype(f32), axis=0
    )
    hidden_grad = lax.ppermute(hidden_grad.T, both, sum_turn(nz))

    my_gain = lax.dynamic_slice_in_dim(norm_gain, dp_index * block, block, 0)
    turned_rms, turned_inner = turned_rows[0][:, None], turned_rows[1][:, None]
    scaled_grad = my_gain[None, :] * hidden_grad
    turned_resid = turned_rms * (
        scaled_grad - turned_stream.astype(f32) * turned_rms * turned_inner
    )
    stream_grad = turned_resid.astype(bf16)
    resid_grad = lax.ppermute(turned_resid, both, turn)

    all_rows = lax.all_to_all(
        jnp.broadcast_to(stream_grad[None], (mp_count, tokens, block)), "mp", 0, 0, tiled=True
    )
    gate = pl.pallas_call(
        gate_kernel,
        out_shape=jax.ShapeDtypeStruct((mp_count, per_expert * capacity), f32),
        compiler_params=pltpu.CompilerParams(vmem_limit_bytes=32 * 1024 * 1024),
    )(turned_slots, stream_grad, turned_proj)
    gate = lax.ppermute(gate, both, turn)
    gate, all_rows, resid_grad = lax.optimization_barrier((gate, all_rows, resid_grad))
    down_grad = pl.pallas_call(
        down_kernel,
        grid_spec=pltpu.PrefetchScalarGridSpec(
            num_scalar_prefetch=1,
            grid=(per_expert,),
            in_specs=[
                pl.BlockSpec((dp_count, tokens, block), lambda e, group: (0, 0, 0)),
            ]
            + [
                pl.BlockSpec(
                    (piece.shape[0], capacity, lanes),
                    lambda e, group: (0, 0, hidden_width // lanes),
                )
                for piece in acts_pieces
            ]
            + acts_specs,
            out_specs=pl.BlockSpec((1, hidden_width, block), lambda e, group: (e, 0, 0)),
            scratch_shapes=[pltpu.VMEM((per_expert, dp_count, capacity, block), bf16)],
        ),
        out_shape=jax.ShapeDtypeStruct((per_expert, hidden_width, block), bf16),
        compiler_params=pltpu.CompilerParams(vmem_limit_bytes=58 * 1024 * 1024),
    )(group_of, all_rows, *acts_pieces, *acts_pieces)

    slot_gate = jnp.sum(
        lax.all_to_all(
            jnp.broadcast_to(gate[None], (mp_count,) + gate.shape), "mp", 0, 0, tiled=True
        ),
        axis=0,
    ).reshape(experts_all, capacity)
    per_token = jnp.sum(jnp.where(matches, slot_gate[:, :, None], 0.0), axis=1)
    gate_grad = jnp.sum(jnp.where(hit_routes, per_token.T[:, None, :], 0.0), axis=2)
    return (resid_grad, down_grad, gate_grad)


def solution(mesh):
    placed = (
        P("dp", None),
        P(),
        P("dp", "mp"),
        P("dp"),
        P("dp"),
        P("dp"),
        P("dp"),
        P("dp", None),
        P("dp", None),
        P("mp", "dp", None, None),
        P("mp", None, "dp"),
    )
    return jax.shard_map(
        local,
        mesh=mesh,
        in_specs=placed,
        out_specs=(P("dp", "mp"), P("mp", None, "dp"), P("dp", None)),
        check_vma=False,
    )
```

```python
import functools

import jax
import jax.numpy as jnp
from jax import lax
from jax.experimental import pallas as pl
from jax.experimental.pallas import tpu as pltpu
from jax.sharding import PartitionSpec as P

clip_low = 0.8
clip_high = 1.2
norm_eps = 1e-06
f32 = jnp.float32
bf16 = jnp.bfloat16
lanes = 128


def z_shift(step, nz):
    return [(2 * z + c, 2 * ((z + step) % nz) + c) for z in range(nz) for c in range(2)]


def core_swap(nz):
    return [(2 * z + c, 2 * z + 1 - c) for z in range(nz) for c in range(2)]


def home_turn(nz):
    return [
        ((2 * z + c) * 16 + 2 * b + low, (2 * z + low) * 16 + 2 * b + c)
        for z in range(nz) for c in range(2) for b in range(nz) for low in range(2)
    ]


def sum_turn(nz):
    return [
        ((2 * z + c) * 16 + 2 * b + low, (2 * b + c) * 16 + 2 * z + low)
        for z in range(nz) for c in range(2) for b in range(nz) for low in range(2)
    ]


def proj_kernel(acts_ref, down_ref, proj_ref):
    groups, _, slots, wide = acts_ref.shape
    acts = acts_ref[:, 0].reshape(groups * slots, wide)
    out = jnp.dot(acts, down_ref[0], preferred_element_type=f32)
    proj_ref[...] = out.astype(proj_ref.dtype).reshape(proj_ref.shape)


def slot_kernel(side_ref, rows_ref, proj_ref, weighted_ref, gate_ref):
    groups, per_expert, slots, _ = side_ref.shape
    tokens, width = rows_ref.shape[1:]
    count = per_expert * slots
    column = lax.broadcasted_iota(jnp.int32, (count, tokens), 1)
    gates = jnp.zeros((count, lanes), f32)
    for group in range(groups):
        side = side_ref[group].reshape(count, lanes).astype(f32)
        match = jnp.where(column.astype(f32) == side[:, 1:2], 1.0, 0.0).astype(bf16)
        rows = jnp.dot(match, rows_ref[group], preferred_element_type=f32)
        proj = proj_ref[group].reshape(count, width)
        gate = jnp.sum(rows * proj, axis=1, keepdims=True)
        gates = jnp.where(column == group, gate, gates)
        weighted = (side[:, 0:1] * rows).astype(bf16)
        weighted_ref[:, group] = weighted.reshape(per_expert, slots, width)
    gate_ref[...] = gates.T[:groups]


def hidden_kernel(nz, place_ref, grad_ref, *refs):
    pieces, out_ref = refs[: nz + 1], refs[nz + 1]
    z_index, core = place_ref[0], place_ref[1]
    tokens = grad_ref.shape[0] // 2
    half = pieces[0].shape[0] // 2
    grad = grad_ref[...]
    for number in range(nz + 1):
        step = (number + 1) // 2
        offset = step if number % 2 == 0 else nz - step
        first = 0
        if number >= nz - 1:
            offset, first = nz // 2, half * (number - nz + 1)
        part = lax.dot_general(
            pieces[number][...], grad, (((1,), (1,)), ((), ())), preferred_element_type=f32
        ).astype(out_ref.dtype)
        rows = slice(first, first + part.shape[0])
        block = lax.rem(z_index + offset, nz)
        out_ref[2 * block + core, rows] = part[:, :tokens]
        out_ref[2 * block + 1 - core, rows] = part[:, tokens:]


def down_kernel(acts_ref, weighted_ref, out_ref):
    groups, _, slots, wide = acts_ref.shape
    acts = acts_ref[:, 0].reshape(groups * slots, wide)
    weighted = weighted_ref[0].reshape(groups * slots, weighted_ref.shape[3])
    out_ref[0] = lax.dot_general(
        acts, weighted, (((0,), (0,)), ((), ())), preferred_element_type=f32
    ).astype(bf16)


def local(
    residual,
    norm_gain,
    head_weight,
    token_ids,
    old_logp,
    advantages,
    resp_mask,
    routes,
    combine_weights,
    expert_acts,
    down_weight,
):
    tokens, model_width = residual.shape
    block, vocab_dev = head_weight.shape
    per_expert, _, capacity, hidden_width = expert_acts.shape
    dp_count = lax.axis_size("dp")
    mp_count = lax.axis_size("mp")
    nz = dp_count // 2
    dp_index = lax.axis_index("dp")
    mp_index = lax.axis_index("mp")
    z_index, core = dp_index // 2, dp_index % 2
    both = ("dp", "mp")
    experts_all = per_expert * mp_count
    swap = functools.partial(lax.ppermute, axis_name="dp", perm=core_swap(nz))

    stream = residual.astype(f32)
    inv_rms = lax.rsqrt(jnp.mean(stream * stream, axis=1, keepdims=True) + norm_eps)
    normed = (stream * inv_rms * norm_gain[None, :]).astype(bf16)
    by_block = normed.reshape(tokens, nz, 2, block).transpose(2, 1, 0, 3)
    mine = lax.dynamic_index_in_dim(by_block, core, 0, keepdims=False)
    theirs = lax.dynamic_index_in_dim(by_block, 1 - core, 0, keepdims=False)
    chip_normed = jnp.concatenate([mine, swap(theirs)], axis=1)

    low = mp_index % 2
    landed_block = mp_index - low + core
    other_stream = swap(
        lax.dynamic_slice_in_dim(residual, (mp_index - low + 1 - core) * block, block, 1)
    )
    landed_stream = jnp.where(
        low == core, lax.dynamic_slice_in_dim(residual, landed_block * block, block, 1), other_stream
    )

    expert_ids = jnp.arange(experts_all, dtype=jnp.int32)
    hit_routes = routes[:, :, None] == expert_ids[None, None, :]
    hit_token = jnp.sum(hit_routes.astype(jnp.int32), axis=1)
    before = jnp.cumsum(hit_token, axis=0) - hit_token
    slot_ids = jnp.arange(capacity, dtype=jnp.int32)
    matches = (hit_token.T[:, None, :] == 1) & (before.T[:, None, :] == slot_ids[None, :, None])
    weight_token = jnp.sum(
        jnp.where(hit_routes, combine_weights[:, :, None].astype(f32), 0.0), axis=1
    )
    first_expert = mp_index * per_expert
    own_matches = lax.dynamic_slice_in_dim(matches, first_expert, per_expert, 0)
    own_weights = lax.dynamic_slice_in_dim(weight_token, first_expert, per_expert, 1)
    token_numbers = jnp.arange(tokens, dtype=jnp.int32)
    slot_token = jnp.sum(jnp.where(own_matches, token_numbers[None, None, :] + 1, 0), axis=2) - 1
    slot_weight = jnp.sum(jnp.where(own_matches, own_weights.T[:, None, :], 0.0), axis=2)
    lane = jnp.arange(lanes, dtype=jnp.int32)
    side = jnp.where(
        lane == 0,
        slot_weight[:, :, None],
        jnp.where(lane == 1, slot_token.astype(f32)[:, :, None], 0.0),
    ).astype(bf16)
    acts_block = jnp.concatenate([expert_acts[:, 0], side], axis=2)

    def logits_of(rows, offset, first, piece):
        features = lax.dynamic_index_in_dim(
            chip_normed, lax.rem(z_index + offset, nz), 0, keepdims=False
        )[rows, first : first + piece.shape[0]]
        return jnp.dot(features, piece, preferred_element_type=f32)

    everything = slice(0, 2 * tokens)
    ahead = lax.ppermute(head_weight, "dp", z_shift(1, nz))
    back = lax.ppermute(head_weight, "dp", z_shift(-1, nz))
    head_pieces = [(0, 0, head_weight), (nz - 1, 0, ahead), (1, 0, back)]
    back, chip_normed, landed_stream, acts_block = lax.optimization_barrier(
        (back, chip_normed, landed_stream, acts_block)
    )
    partial, used = None, 0
    for step in range(2, nz // 2):
        if step > 2:
            back, partial = lax.optimization_barrier((back, partial))
        for piece in head_pieces[used:]:
            added = logits_of(everything, *piece)
            partial = added if partial is None else partial + added
        used = len(head_pieces)
        ahead = lax.ppermute(ahead, "dp", z_shift(1, nz))
        back = lax.ppermute(back, "dp", z_shift(-1, nz))
        head_pieces += [(nz - step, 0, ahead), (step, 0, back)]
    back, partial = lax.optimization_barrier((back, partial))
    half = block // 2
    last_pieces = [
        (nz // 2, 0, lax.ppermute(ahead[:half], "dp", z_shift(1, nz))),
        (nz // 2, half, lax.ppermute(back[half:], "dp", z_shift(-1, nz))),
    ]
    for piece in head_pieces[used:]:
        partial = partial + logits_of(everything, *piece)
    own_part, other_part = partial[:tokens], partial[tokens:]
    for piece in last_pieces:
        other_part = other_part + logits_of(slice(tokens, None), *piece)
        own_part = own_part + logits_of(slice(0, tokens), *piece)
    head_pieces += last_pieces
    logits = own_part + swap(other_part)

    acts_block, _ = lax.optimization_barrier((acts_block, tuple(p for _, _, p in last_pieces)))
    acts_all = lax.all_gather(acts_block, "dp", axis=0, tiled=False)
    proj = pl.pallas_call(
        proj_kernel,
        grid=(per_expert,),
        in_specs=[
            pl.BlockSpec((dp_count, 1, capacity, hidden_width), lambda e: (0, e, 0, 0)),
            pl.BlockSpec((1, hidden_width, block), lambda e: (e, 0, 0)),
        ],
        out_specs=pl.BlockSpec((dp_count, 1, capacity, block), lambda e: (0, e, 0, 0)),
        out_shape=jax.ShapeDtypeStruct((dp_count, per_expert, capacity, block), f32),
        compiler_params=pltpu.CompilerParams(vmem_limit_bytes=58 * 1024 * 1024),
    )(acts_all, down_weight)

    local_ids = token_ids - mp_index * vocab_dev
    column = jnp.arange(vocab_dev, dtype=jnp.int32)
    onehot = column[None, :] == local_ids[:, None]
    local_top = jnp.max(logits, axis=1)
    local_exp = jnp.exp(logits - local_top[:, None])
    local_total = jnp.sum(local_exp, axis=1)
    local_mean = jnp.sum(local_exp * logits, axis=1)
    local_picked = jnp.sum(jnp.where(onehot, logits, 0.0), axis=1)
    stats = jnp.stack([local_top, local_total, local_mean, local_picked])
    stats = lax.all_to_all(
        jnp.broadcast_to(stats[None], (mp_count, 4, tokens)), "mp", 0, 0, tiled=True
    )
    row_top = jnp.max(stats[:, 0], axis=0)
    rescale = jnp.exp(stats[:, 0] - row_top[None])
    row_total = jnp.sum(stats[:, 1] * rescale, axis=0)
    mean_logit = jnp.sum(stats[:, 2] * rescale, axis=0) / row_total
    picked = jnp.sum(stats[:, 3], axis=0)

    logp = picked - row_top - jnp.log(row_total)
    prob_ratio = jnp.exp(logp - old_logp)
    weight_row = -jnp.clip(prob_ratio, clip_low, clip_high) * advantages * resp_mask.astype(f32)
    inner = weight_row * (picked - mean_logit) / model_width
    own_rows = jnp.stack([inv_rms[:, 0], inner])
    landed_rows = jnp.where(low == core, own_rows, swap(own_rows))
    logit_grad = (
        weight_row[:, None]
        * (onehot.astype(f32) - jnp.exp(logits - row_top[:, None]) / row_total[:, None])
    ).astype(bf16)
    chip_grad = jnp.concatenate([logit_grad, swap(logit_grad)], axis=0)

    place = jnp.stack([z_index, core]).astype(jnp.int32)
    hidden = pl.pallas_call(
        functools.partial(hidden_kernel, nz),
        in_specs=[pl.BlockSpec(memory_space=pltpu.SMEM)]
        + [pl.BlockSpec(memory_space=pltpu.VMEM)] * (nz + 2),
        out_specs=pl.BlockSpec(memory_space=pltpu.VMEM),
        out_shape=jax.ShapeDtypeStruct((mp_count, block, tokens), f32),
        compiler_params=pltpu.CompilerParams(vmem_limit_bytes=40 * 1024 * 1024),
    )(place, chip_grad, *[piece for _, _, piece in head_pieces])

    hidden = lax.all_to_all(hidden, "mp", 0, 0, tiled=True)
    hidden_grad = jnp.sum(hidden, axis=0).T

    landed_gain = lax.dynamic_slice_in_dim(norm_gain, landed_block * block, block, 0)
    landed_rms, landed_inner = landed_rows[0][:, None], landed_rows[1][:, None]
    scaled_grad = landed_gain[None, :] * hidden_grad
    landed_resid = landed_rms * (
        scaled_grad - landed_stream.astype(f32) * landed_rms * landed_inner
    )
    resid_grad = lax.ppermute(landed_resid, both, home_turn(nz))
    stream_grad = lax.ppermute(landed_resid.astype(bf16), both, sum_turn(nz))

    all_rows = lax.all_to_all(
        jnp.broadcast_to(stream_grad[None], (mp_count, tokens, block)), "mp", 0, 0, tiled=True
    )
    all_rows, resid_grad, proj = lax.optimization_barrier((all_rows, resid_grad, proj))
    weighted, gate = pl.pallas_call(
        slot_kernel,
        grid=(1,),
        in_specs=[
            pl.BlockSpec(
                (dp_count, per_expert, capacity, lanes), lambda n: (0, 0, 0, hidden_width // lanes)
            ),
            pl.BlockSpec((dp_count, tokens, block), lambda n: (0, 0, 0)),
            pl.BlockSpec((dp_count, per_expert, capacity, block), lambda n: (0, 0, 0, 0)),
        ],
        out_specs=[
            pl.BlockSpec((per_expert, dp_count, capacity, block), lambda n: (0, 0, 0, 0)),
            pl.BlockSpec((dp_count, per_expert * capacity), lambda n: (0, 0)),
        ],
        out_shape=[
            jax.ShapeDtypeStruct((per_expert, dp_count, capacity, block), bf16),
            jax.ShapeDtypeStruct((dp_count, per_expert * capacity), f32),
        ],
        compiler_params=pltpu.CompilerParams(vmem_limit_bytes=56 * 1024 * 1024),
    )(acts_all, all_rows, proj)
    down_grad = pl.pallas_call(
        down_kernel,
        grid=(per_expert,),
        in_specs=[
            pl.BlockSpec((dp_count, 1, capacity, hidden_width), lambda e: (0, e, 0, 0)),
            pl.BlockSpec((1, dp_count, capacity, block), lambda e: (e, 0, 0, 0)),
        ],
        out_specs=pl.BlockSpec((1, hidden_width, block), lambda e: (e, 0, 0)),
        out_shape=jax.ShapeDtypeStruct((per_expert, hidden_width, block), bf16),
        compiler_params=pltpu.CompilerParams(vmem_limit_bytes=56 * 1024 * 1024),
    )(acts_all, weighted)

    gate = lax.all_to_all(
        jnp.broadcast_to(gate[:, None, :], (dp_count, mp_count, per_expert * capacity)).reshape(
            dp_count * mp_count, 1, per_expert * capacity
        ),
        both, 0, 0, tiled=True,
    ).reshape(dp_count, mp_count, per_expert * capacity)
    slot_gate = jnp.sum(gate, axis=0).reshape(experts_all, capacity)
    per_token = jnp.sum(jnp.where(matches, slot_gate[:, :, None], 0.0), axis=1)
    gate_grad = jnp.sum(jnp.where(hit_routes, per_token.T[:, None, :], 0.0), axis=2)
    return (resid_grad, down_grad, gate_grad)


def solution(mesh):
    placed = (
        P("dp", None),
        P(),
        P("dp", "mp"),
        P("dp"),
        P("dp"),
        P("dp"),
        P("dp"),
        P("dp", None),
        P("dp", None),
        P("mp", "dp", None, None),
        P("mp", None, "dp"),
    )
    return jax.shard_map(
        local,
        mesh=mesh,
        in_specs=placed,
        out_specs=(P("dp", "mp"), P("mp", None, "dp"), P("dp", None)),
        check_vma=False,
    )
```

```python
import functools

import jax
import jax.numpy as jnp
from jax import lax
from jax.experimental import pallas as pl
from jax.experimental.pallas import tpu as pltpu
from jax.sharding import PartitionSpec as P

clip_low = 0.8
clip_high = 1.2
norm_eps = 1e-06
f32 = jnp.float32
bf16 = jnp.bfloat16
lanes = 128


def z_shift(step, nz):
    return [(2 * z + c, 2 * ((z + step) % nz) + c) for z in range(nz) for c in range(2)]


def core_swap(nz):
    return [(2 * z + c, 2 * z + 1 - c) for z in range(nz) for c in range(2)]


def home_turn(nz):
    return [
        ((2 * z + c) * 16 + 2 * b + low, (2 * z + low) * 16 + 2 * b + c)
        for z in range(nz) for c in range(2) for b in range(nz) for low in range(2)
    ]


def sum_turn(nz):
    return [
        ((2 * z + c) * 16 + 2 * b + low, (2 * b + c) * 16 + 2 * z + low)
        for z in range(nz) for c in range(2) for b in range(nz) for low in range(2)
    ]


def proj_kernel(acts_ref, down_ref, proj_ref):
    groups, _, slots, wide = acts_ref.shape
    acts = acts_ref[:, 0].reshape(groups * slots, wide)
    out = jnp.dot(acts, down_ref[0], preferred_element_type=f32)
    proj_ref[...] = out.astype(proj_ref.dtype).reshape(proj_ref.shape)


def slot_kernel(side_ref, rows_ref, proj_ref, weighted_ref, gate_ref):
    groups, per_expert, slots, _ = side_ref.shape
    tokens, width = rows_ref.shape[1:]
    count = per_expert * slots
    column = lax.broadcasted_iota(jnp.int32, (count, tokens), 1)
    gates = jnp.zeros((count, lanes), f32)
    for group in range(groups):
        side = side_ref[group].reshape(count, lanes).astype(f32)
        match = jnp.where(column.astype(f32) == side[:, 1:2], 1.0, 0.0).astype(bf16)
        rows = jnp.dot(match, rows_ref[group], preferred_element_type=f32)
        proj = proj_ref[group].reshape(count, width)
        gate = jnp.sum(rows * proj, axis=1, keepdims=True)
        gates = jnp.where(column == group, gate, gates)
        weighted = (side[:, 0:1] * rows).astype(bf16)
        weighted_ref[:, group] = weighted.reshape(per_expert, slots, width)
    gate_ref[...] = gates.T[:groups]


def hidden_kernel(nz, place_ref, grad_ref, *refs):
    pieces, out_ref = refs[: nz + 1], refs[nz + 1]
    z_index, core = place_ref[0], place_ref[1]
    tokens = grad_ref.shape[0] // 2
    half = pieces[0].shape[0] // 2
    grad = grad_ref[...]
    for number in range(nz + 1):
        step = (number + 1) // 2
        offset = step if number % 2 == 0 else nz - step
        first = 0
        if number >= nz - 1:
            offset, first = nz // 2, half * (number - nz + 1)
        part = lax.dot_general(
            pieces[number][...], grad, (((1,), (1,)), ((), ())), preferred_element_type=f32
        ).astype(out_ref.dtype)
        rows = slice(first, first + part.shape[0])
        block = lax.rem(z_index + offset, nz)
        out_ref[2 * block + core, rows] = part[:, :tokens]
        out_ref[2 * block + 1 - core, rows] = part[:, tokens:]


def down_kernel(acts_ref, weighted_ref, out_ref):
    groups, _, slots, wide = acts_ref.shape
    acts = acts_ref[:, 0].reshape(groups * slots, wide)
    weighted = weighted_ref[0].reshape(groups * slots, weighted_ref.shape[3])
    out_ref[0] = lax.dot_general(
        acts, weighted, (((0,), (0,)), ((), ())), preferred_element_type=f32
    ).astype(bf16)


def local(
    residual,
    norm_gain,
    head_weight,
    token_ids,
    old_logp,
    advantages,
    resp_mask,
    routes,
    combine_weights,
    expert_acts,
    down_weight,
):
    tokens, model_width = residual.shape
    block, vocab_dev = head_weight.shape
    per_expert, _, capacity, hidden_width = expert_acts.shape
    dp_count = lax.axis_size("dp")
    mp_count = lax.axis_size("mp")
    nz = dp_count // 2
    dp_index = lax.axis_index("dp")
    mp_index = lax.axis_index("mp")
    z_index, core = dp_index // 2, dp_index % 2
    both = ("dp", "mp")
    experts_all = per_expert * mp_count
    swap = functools.partial(lax.ppermute, axis_name="dp", perm=core_swap(nz))

    stream = residual.astype(f32)
    inv_rms = lax.rsqrt(jnp.mean(stream * stream, axis=1, keepdims=True) + norm_eps)
    normed = (stream * inv_rms * norm_gain[None, :]).astype(bf16)
    by_block = normed.reshape(tokens, nz, 2, block).transpose(2, 1, 0, 3)
    mine = lax.dynamic_index_in_dim(by_block, core, 0, keepdims=False)
    theirs = lax.dynamic_index_in_dim(by_block, 1 - core, 0, keepdims=False)
    chip_normed = jnp.concatenate([mine, swap(theirs)], axis=1)

    low = mp_index % 2
    landed_block = mp_index - low + core
    other_stream = swap(
        lax.dynamic_slice_in_dim(residual, (mp_index - low + 1 - core) * block, block, 1)
    )
    landed_stream = jnp.where(
        low == core, lax.dynamic_slice_in_dim(residual, landed_block * block, block, 1), other_stream
    )

    expert_ids = jnp.arange(experts_all, dtype=jnp.int32)
    hit_routes = routes[:, :, None] == expert_ids[None, None, :]
    hit_token = jnp.sum(hit_routes.astype(jnp.int32), axis=1)
    before = jnp.cumsum(hit_token, axis=0) - hit_token
    slot_ids = jnp.arange(capacity, dtype=jnp.int32)
    matches = (hit_token.T[:, None, :] == 1) & (before.T[:, None, :] == slot_ids[None, :, None])
    weight_token = jnp.sum(
        jnp.where(hit_routes, combine_weights[:, :, None].astype(f32), 0.0), axis=1
    )
    first_expert = mp_index * per_expert
    own_matches = lax.dynamic_slice_in_dim(matches, first_expert, per_expert, 0)
    own_weights = lax.dynamic_slice_in_dim(weight_token, first_expert, per_expert, 1)
    token_numbers = jnp.arange(tokens, dtype=jnp.int32)
    slot_token = jnp.sum(jnp.where(own_matches, token_numbers[None, None, :] + 1, 0), axis=2) - 1
    slot_weight = jnp.sum(jnp.where(own_matches, own_weights.T[:, None, :], 0.0), axis=2)
    lane = jnp.arange(lanes, dtype=jnp.int32)
    side = jnp.where(
        lane == 0,
        slot_weight[:, :, None],
        jnp.where(lane == 1, slot_token.astype(f32)[:, :, None], 0.0),
    ).astype(bf16)
    acts_block = jnp.concatenate([expert_acts[:, 0], side], axis=2)

    def logits_of(rows, offset, first, piece):
        features = lax.dynamic_index_in_dim(
            chip_normed, lax.rem(z_index + offset, nz), 0, keepdims=False
        )[rows, first : first + piece.shape[0]]
        return jnp.dot(features, piece, preferred_element_type=f32)

    everything = slice(0, 2 * tokens)
    ahead = lax.ppermute(head_weight, "dp", z_shift(1, nz))
    back = lax.ppermute(head_weight, "dp", z_shift(-1, nz))
    head_pieces = [(0, 0, head_weight), (nz - 1, 0, ahead), (1, 0, back)]
    back, chip_normed, landed_stream, acts_block = lax.optimization_barrier(
        (back, chip_normed, landed_stream, acts_block)
    )
    partial, used = None, 0
    for step in range(2, nz // 2):
        if step > 2:
            back, partial = lax.optimization_barrier((back, partial))
        for piece in head_pieces[used:]:
            added = logits_of(everything, *piece)
            partial = added if partial is None else partial + added
        used = len(head_pieces)
        ahead = lax.ppermute(ahead, "dp", z_shift(1, nz))
        back = lax.ppermute(back, "dp", z_shift(-1, nz))
        head_pieces += [(nz - step, 0, ahead), (step, 0, back)]
    back, partial = lax.optimization_barrier((back, partial))
    half = block // 2
    last_pieces = [
        (nz // 2, 0, lax.ppermute(ahead[:half], "dp", z_shift(1, nz))),
        (nz // 2, half, lax.ppermute(back[half:], "dp", z_shift(-1, nz))),
    ]
    for piece in head_pieces[used:]:
        partial = partial + logits_of(everything, *piece)
    own_part, other_part = partial[:tokens], partial[tokens:]
    for piece in last_pieces:
        other_part = other_part + logits_of(slice(tokens, None), *piece)
        own_part = own_part + logits_of(slice(0, tokens), *piece)
    head_pieces += last_pieces
    logits = own_part + swap(other_part)

    acts_block, _ = lax.optimization_barrier((acts_block, tuple(p for _, _, p in last_pieces)))
    acts_all = lax.all_gather(acts_block, "dp", axis=0, tiled=False)
    proj = pl.pallas_call(
        proj_kernel,
        grid=(per_expert,),
        in_specs=[
            pl.BlockSpec((dp_count, 1, capacity, hidden_width), lambda e: (0, e, 0, 0)),
            pl.BlockSpec((1, hidden_width, block), lambda e: (e, 0, 0)),
        ],
        out_specs=pl.BlockSpec((dp_count, 1, capacity, block), lambda e: (0, e, 0, 0)),
        out_shape=jax.ShapeDtypeStruct((dp_count, per_expert, capacity, block), f32),
        compiler_params=pltpu.CompilerParams(vmem_limit_bytes=58 * 1024 * 1024),
    )(acts_all, down_weight)

    local_ids = token_ids - mp_index * vocab_dev
    column = jnp.arange(vocab_dev, dtype=jnp.int32)
    onehot = column[None, :] == local_ids[:, None]
    local_top = jnp.max(logits, axis=1)
    local_exp = jnp.exp(logits - local_top[:, None])
    local_total = jnp.sum(local_exp, axis=1)
    local_mean = jnp.sum(local_exp * logits, axis=1)
    local_picked = jnp.sum(jnp.where(onehot, logits, 0.0), axis=1)
    stats = jnp.stack([local_top, local_total, local_mean, local_picked])
    stats = lax.all_to_all(
        jnp.broadcast_to(stats[None], (mp_count, 4, tokens)), "mp", 0, 0, tiled=True
    )
    row_top = jnp.max(stats[:, 0], axis=0)
    rescale = jnp.exp(stats[:, 0] - row_top[None])
    row_total = jnp.sum(stats[:, 1] * rescale, axis=0)
    mean_logit = jnp.sum(stats[:, 2] * rescale, axis=0) / row_total
    picked = jnp.sum(stats[:, 3], axis=0)

    logp = picked - row_top - jnp.log(row_total)
    prob_ratio = jnp.exp(logp - old_logp)
    weight_row = -jnp.clip(prob_ratio, clip_low, clip_high) * advantages * resp_mask.astype(f32)
    inner = weight_row * (picked - mean_logit) / model_width
    own_rows = jnp.stack([inv_rms[:, 0], inner])
    landed_rows = jnp.where(low == core, own_rows, swap(own_rows))
    logit_grad = (
        weight_row[:, None]
        * (onehot.astype(f32) - jnp.exp(logits - row_top[:, None]) / row_total[:, None])
    ).astype(bf16)
    chip_grad = jnp.concatenate([logit_grad, swap(logit_grad)], axis=0)

    place = jnp.stack([z_index, core]).astype(jnp.int32)
    hidden = pl.pallas_call(
        functools.partial(hidden_kernel, nz),
        in_specs=[pl.BlockSpec(memory_space=pltpu.SMEM)]
        + [pl.BlockSpec(memory_space=pltpu.VMEM)] * (nz + 2),
        out_specs=pl.BlockSpec(memory_space=pltpu.VMEM),
        out_shape=jax.ShapeDtypeStruct((mp_count, block, tokens), f32),
        compiler_params=pltpu.CompilerParams(vmem_limit_bytes=40 * 1024 * 1024),
    )(place, chip_grad, *[piece for _, _, piece in head_pieces])

    hidden = lax.all_to_all(hidden, "mp", 0, 0, tiled=True)
    side_all = acts_all[..., hidden_width:]
    hidden, proj, side_all, landed_rows = lax.optimization_barrier(
        (hidden, proj, side_all, landed_rows)
    )
    hidden_grad = jnp.sum(hidden, axis=0).T

    landed_gain = lax.dynamic_slice_in_dim(norm_gain, landed_block * block, block, 0)
    landed_rms, landed_inner = landed_rows[0][:, None], landed_rows[1][:, None]
    scaled_grad = landed_gain[None, :] * hidden_grad
    landed_resid = landed_rms * (
        scaled_grad - landed_stream.astype(f32) * landed_rms * landed_inner
    )
    stream_grad = lax.ppermute(landed_resid.astype(bf16), both, sum_turn(nz))
    resid_grad = lax.ppermute(landed_resid, both, home_turn(nz))
    stream_grad, resid_grad = lax.optimization_barrier((stream_grad, resid_grad))

    all_rows = lax.all_to_all(
        jnp.broadcast_to(stream_grad[None], (mp_count, tokens, block)), "mp", 0, 0, tiled=True
    )
    weighted, gate = pl.pallas_call(
        slot_kernel,
        in_specs=[pl.BlockSpec(memory_space=pltpu.VMEM)] * 3,
        out_specs=[pl.BlockSpec(memory_space=pltpu.VMEM)] * 2,
        out_shape=[
            jax.ShapeDtypeStruct((per_expert, dp_count, capacity, block), bf16),
            jax.ShapeDtypeStruct((dp_count, per_expert * capacity), f32),
        ],
        compiler_params=pltpu.CompilerParams(vmem_limit_bytes=32 * 1024 * 1024),
    )(side_all, all_rows, proj)
    down_grad = pl.pallas_call(
        down_kernel,
        grid=(per_expert,),
        in_specs=[
            pl.BlockSpec((dp_count, 1, capacity, hidden_width), lambda e: (0, e, 0, 0)),
            pl.BlockSpec((1, dp_count, capacity, block), lambda e: (e, 0, 0, 0)),
        ],
        out_specs=pl.BlockSpec((1, hidden_width, block), lambda e: (e, 0, 0)),
        out_shape=jax.ShapeDtypeStruct((per_expert, hidden_width, block), bf16),
        compiler_params=pltpu.CompilerParams(vmem_limit_bytes=56 * 1024 * 1024),
    )(acts_all, weighted)

    gate = lax.all_to_all(
        jnp.broadcast_to(gate[:, None, :], (dp_count, mp_count, per_expert * capacity)).reshape(
            dp_count * mp_count, 1, per_expert * capacity
        ),
        both, 0, 0, tiled=True,
    ).reshape(dp_count, mp_count, per_expert * capacity)
    slot_gate = jnp.sum(gate, axis=0).reshape(experts_all, capacity)
    per_token = jnp.sum(jnp.where(matches, slot_gate[:, :, None], 0.0), axis=1)
    gate_grad = jnp.sum(jnp.where(hit_routes, per_token.T[:, None, :], 0.0), axis=2)
    return (resid_grad, down_grad, gate_grad)


def solution(mesh):
    placed = (
        P("dp", None),
        P(),
        P("dp", "mp"),
        P("dp"),
        P("dp"),
        P("dp"),
        P("dp"),
        P("dp", None),
        P("dp", None),
        P("mp", "dp", None, None),
        P("mp", None, "dp"),
    )
    return jax.shard_map(
        local,
        mesh=mesh,
        in_specs=placed,
        out_specs=(P("dp", "mp"), P("mp", None, "dp"), P("dp", None)),
        check_vma=False,
    )
```

```python
import functools

import jax
import jax.numpy as jnp
from jax import lax
from jax.experimental import pallas as pl
from jax.experimental.pallas import tpu as pltpu
from jax.sharding import PartitionSpec as P

clip_low = 0.8
clip_high = 1.2
norm_eps = 1e-06
f32 = jnp.float32
bf16 = jnp.bfloat16
lanes = 128


def z_shift(step, nz):
    return [(2 * z + c, 2 * ((z + step) % nz) + c) for z in range(nz) for c in range(2)]


def core_swap(nz):
    return [(2 * z + c, 2 * z + 1 - c) for z in range(nz) for c in range(2)]


def home_turn(nz):
    return [
        ((2 * z + c) * 16 + 2 * b + low, (2 * z + low) * 16 + 2 * b + c)
        for z in range(nz) for c in range(2) for b in range(nz) for low in range(2)
    ]


def sum_turn(nz):
    return [
        ((2 * z + c) * 16 + 2 * b + low, (2 * b + c) * 16 + 2 * z + low)
        for z in range(nz) for c in range(2) for b in range(nz) for low in range(2)
    ]


def proj_kernel(acts_ref, down_ref, proj_ref):
    groups, _, slots, wide = acts_ref.shape
    acts = acts_ref[:, 0].reshape(groups * slots, wide)
    out = jnp.dot(acts, down_ref[0], preferred_element_type=f32)
    proj_ref[...] = out.astype(proj_ref.dtype).reshape(proj_ref.shape)


def gate_kernel(side_ref, rows_ref, proj_ref, gate_ref):
    groups, per_expert, slots, _ = side_ref.shape
    tokens, width = rows_ref.shape[1:]
    count = per_expert * slots
    column = lax.broadcasted_iota(jnp.int32, (count, tokens), 1)
    gates = jnp.zeros((count, lanes), f32)
    for group in range(groups):
        token = side_ref[group].reshape(count, lanes)[:, 1:2].astype(f32)
        match = jnp.where(column.astype(f32) == token, 1.0, 0.0).astype(bf16)
        rows = jnp.dot(match, rows_ref[group], preferred_element_type=f32)
        gate = jnp.sum(rows * proj_ref[group].reshape(count, width), axis=1, keepdims=True)
        gates = jnp.where(column == group, gate, gates)
    gates = gates.T
    for group in range(groups):
        gate_ref[group] = jnp.broadcast_to(gates[group : group + 1], gate_ref.shape[1:])


def hidden_kernel(nz, place_ref, grad_ref, *refs):
    pieces, out_ref = refs[: nz + 1], refs[nz + 1]
    z_index, core = place_ref[0], place_ref[1]
    tokens = grad_ref.shape[0] // 2
    half = pieces[0].shape[0] // 2
    grad = grad_ref[...]
    for number in range(nz + 1):
        step = (number + 1) // 2
        offset = step if number % 2 == 0 else nz - step
        first = 0
        if number >= nz - 1:
            offset, first = nz // 2, half * (number - nz + 1)
        part = lax.dot_general(
            pieces[number][...], grad, (((1,), (1,)), ((), ())), preferred_element_type=f32
        ).astype(out_ref.dtype)
        rows = slice(first, first + part.shape[0])
        block = lax.rem(z_index + offset, nz)
        out_ref[2 * block + core, rows] = part[:, :tokens]
        out_ref[2 * block + 1 - core, rows] = part[:, tokens:]


def down_kernel(side_ref, rows_ref, acts_ref, out_ref, weighted):
    groups, per_expert, slots, _ = side_ref.shape
    tokens, width = rows_ref.shape[1:]
    count = per_expert * slots
    expert = pl.program_id(0)

    @pl.when(expert == 0)
    def _():
        column = lax.broadcasted_iota(jnp.int32, (count, tokens), 1).astype(f32)
        for group in range(groups):
            side = side_ref[group].reshape(count, lanes).astype(f32)
            match = jnp.where(column == side[:, 1:2], 1.0, 0.0).astype(bf16)
            rows = jnp.dot(match, rows_ref[group], preferred_element_type=f32)
            made = (side[:, 0:1] * rows).astype(bf16)
            weighted[:, group] = made.reshape(per_expert, slots, width)

    acts = acts_ref[:, 0].reshape(groups * slots, acts_ref.shape[3])
    out_ref[0] = lax.dot_general(
        acts,
        weighted[expert].reshape(groups * slots, width),
        (((0,), (0,)), ((), ())),
        preferred_element_type=f32,
    ).astype(bf16)


def local(
    residual,
    norm_gain,
    head_weight,
    token_ids,
    old_logp,
    advantages,
    resp_mask,
    routes,
    combine_weights,
    expert_acts,
    down_weight,
):
    tokens, model_width = residual.shape
    block, vocab_dev = head_weight.shape
    per_expert, _, capacity, hidden_width = expert_acts.shape
    dp_count = lax.axis_size("dp")
    mp_count = lax.axis_size("mp")
    nz = dp_count // 2
    dp_index = lax.axis_index("dp")
    mp_index = lax.axis_index("mp")
    z_index, core = dp_index // 2, dp_index % 2
    both = ("dp", "mp")
    experts_all = per_expert * mp_count
    swap = functools.partial(lax.ppermute, axis_name="dp", perm=core_swap(nz))

    stream = residual.astype(f32)
    inv_rms = lax.rsqrt(jnp.mean(stream * stream, axis=1, keepdims=True) + norm_eps)
    normed = (stream * inv_rms * norm_gain[None, :]).astype(bf16)
    by_block = normed.reshape(tokens, nz, 2, block).transpose(2, 1, 0, 3)
    mine = lax.dynamic_index_in_dim(by_block, core, 0, keepdims=False)
    theirs = lax.dynamic_index_in_dim(by_block, 1 - core, 0, keepdims=False)
    chip_normed = jnp.concatenate([mine, swap(theirs)], axis=1)

    low = mp_index % 2
    landed_block = mp_index - low + core
    other_stream = swap(
        lax.dynamic_slice_in_dim(residual, (mp_index - low + 1 - core) * block, block, 1)
    )
    landed_stream = jnp.where(
        low == core, lax.dynamic_slice_in_dim(residual, landed_block * block, block, 1), other_stream
    )

    expert_ids = jnp.arange(experts_all, dtype=jnp.int32)
    hit_routes = routes[:, :, None] == expert_ids[None, None, :]
    hit_token = jnp.sum(hit_routes.astype(jnp.int32), axis=1)
    before = jnp.cumsum(hit_token, axis=0) - hit_token
    slot_ids = jnp.arange(capacity, dtype=jnp.int32)
    matches = (hit_token.T[:, None, :] == 1) & (before.T[:, None, :] == slot_ids[None, :, None])
    weight_token = jnp.sum(
        jnp.where(hit_routes, combine_weights[:, :, None].astype(f32), 0.0), axis=1
    )
    first_expert = mp_index * per_expert
    own_matches = lax.dynamic_slice_in_dim(matches, first_expert, per_expert, 0)
    own_weights = lax.dynamic_slice_in_dim(weight_token, first_expert, per_expert, 1)
    token_numbers = jnp.arange(tokens, dtype=jnp.int32)
    slot_token = jnp.sum(jnp.where(own_matches, token_numbers[None, None, :] + 1, 0), axis=2) - 1
    slot_weight = jnp.sum(jnp.where(own_matches, own_weights.T[:, None, :], 0.0), axis=2)
    lane = jnp.arange(lanes, dtype=jnp.int32)
    side = jnp.where(
        lane == 0,
        slot_weight[:, :, None],
        jnp.where(lane == 1, slot_token.astype(f32)[:, :, None], 0.0),
    ).astype(bf16)
    acts_block = jnp.concatenate([expert_acts[:, 0], side], axis=2)

    def logits_of(rows, offset, first, piece):
        features = lax.dynamic_index_in_dim(
            chip_normed, lax.rem(z_index + offset, nz), 0, keepdims=False
        )[rows, first : first + piece.shape[0]]
        return jnp.dot(features, piece, preferred_element_type=f32)

    everything = slice(0, 2 * tokens)
    ahead = lax.ppermute(head_weight, "dp", z_shift(1, nz))
    back = lax.ppermute(head_weight, "dp", z_shift(-1, nz))
    head_pieces = [(0, 0, head_weight), (nz - 1, 0, ahead), (1, 0, back)]
    back, chip_normed, landed_stream, acts_block = lax.optimization_barrier(
        (back, chip_normed, landed_stream, acts_block)
    )
    partial, used = None, 0
    for step in range(2, nz // 2):
        if step > 2:
            back, partial = lax.optimization_barrier((back, partial))
        for piece in head_pieces[used:]:
            added = logits_of(everything, *piece)
            partial = added if partial is None else partial + added
        used = len(head_pieces)
        ahead = lax.ppermute(ahead, "dp", z_shift(1, nz))
        back = lax.ppermute(back, "dp", z_shift(-1, nz))
        head_pieces += [(nz - step, 0, ahead), (step, 0, back)]
    back, partial = lax.optimization_barrier((back, partial))
    half = block // 2
    last_pieces = [
        (nz // 2, 0, lax.ppermute(ahead[:half], "dp", z_shift(1, nz))),
        (nz // 2, half, lax.ppermute(back[half:], "dp", z_shift(-1, nz))),
    ]
    for piece in head_pieces[used:]:
        partial = partial + logits_of(everything, *piece)
    own_part, other_part = partial[:tokens], partial[tokens:]
    for piece in last_pieces:
        other_part = other_part + logits_of(slice(tokens, None), *piece)
        own_part = own_part + logits_of(slice(0, tokens), *piece)
    head_pieces += last_pieces
    logits = own_part + swap(other_part)

    acts_block, _ = lax.optimization_barrier((acts_block, tuple(p for _, _, p in last_pieces)))
    acts_all = lax.all_gather(acts_block, "dp", axis=0, tiled=False)
    proj = pl.pallas_call(
        proj_kernel,
        grid=(per_expert,),
        in_specs=[
            pl.BlockSpec((dp_count, 1, capacity, hidden_width), lambda e: (0, e, 0, 0)),
            pl.BlockSpec((1, hidden_width, block), lambda e: (e, 0, 0)),
        ],
        out_specs=pl.BlockSpec((dp_count, 1, capacity, block), lambda e: (0, e, 0, 0)),
        out_shape=jax.ShapeDtypeStruct((dp_count, per_expert, capacity, block), f32),
        compiler_params=pltpu.CompilerParams(vmem_limit_bytes=58 * 1024 * 1024),
    )(acts_all, down_weight)

    local_ids = token_ids - mp_index * vocab_dev
    column = jnp.arange(vocab_dev, dtype=jnp.int32)
    onehot = column[None, :] == local_ids[:, None]
    local_top = jnp.max(logits, axis=1)
    local_exp = jnp.exp(logits - local_top[:, None])
    local_total = jnp.sum(local_exp, axis=1)
    local_mean = jnp.sum(local_exp * logits, axis=1)
    local_picked = jnp.sum(jnp.where(onehot, logits, 0.0), axis=1)
    stats = jnp.stack([local_top, local_total, local_mean, local_picked])
    stats = lax.all_to_all(
        jnp.broadcast_to(stats[None], (mp_count, 4, tokens)), "mp", 0, 0, tiled=True
    )
    row_top = jnp.max(stats[:, 0], axis=0)
    rescale = jnp.exp(stats[:, 0] - row_top[None])
    row_total = jnp.sum(stats[:, 1] * rescale, axis=0)
    mean_logit = jnp.sum(stats[:, 2] * rescale, axis=0) / row_total
    picked = jnp.sum(stats[:, 3], axis=0)

    logp = picked - row_top - jnp.log(row_total)
    prob_ratio = jnp.exp(logp - old_logp)
    weight_row = -jnp.clip(prob_ratio, clip_low, clip_high) * advantages * resp_mask.astype(f32)
    inner = weight_row * (picked - mean_logit) / model_width
    own_rows = jnp.stack([inv_rms[:, 0], inner])
    landed_rows = jnp.where(low == core, own_rows, swap(own_rows))
    logit_grad = (
        weight_row[:, None]
        * (onehot.astype(f32) - jnp.exp(logits - row_top[:, None]) / row_total[:, None])
    ).astype(bf16)
    chip_grad = jnp.concatenate([logit_grad, swap(logit_grad)], axis=0)

    place = jnp.stack([z_index, core]).astype(jnp.int32)
    hidden = pl.pallas_call(
        functools.partial(hidden_kernel, nz),
        in_specs=[pl.BlockSpec(memory_space=pltpu.SMEM)]
        + [pl.BlockSpec(memory_space=pltpu.VMEM)] * (nz + 2),
        out_specs=pl.BlockSpec(memory_space=pltpu.VMEM),
        out_shape=jax.ShapeDtypeStruct((mp_count, block, tokens), f32),
        compiler_params=pltpu.CompilerParams(vmem_limit_bytes=40 * 1024 * 1024),
    )(place, chip_grad, *[piece for _, _, piece in head_pieces])

    hidden = lax.all_to_all(hidden, "mp", 0, 0, tiled=True)
    side_all = acts_all[..., hidden_width:]
    hidden, proj, side_all, landed_rows = lax.optimization_barrier(
        (hidden, proj, side_all, landed_rows)
    )
    hidden_grad = jnp.sum(hidden, axis=0).T

    landed_gain = lax.dynamic_slice_in_dim(norm_gain, landed_block * block, block, 0)
    landed_rms, landed_inner = landed_rows[0][:, None], landed_rows[1][:, None]
    scaled_grad = landed_gain[None, :] * hidden_grad
    landed_resid = landed_rms * (
        scaled_grad - landed_stream.astype(f32) * landed_rms * landed_inner
    )
    stream_grad = lax.ppermute(landed_resid.astype(bf16), both, sum_turn(nz))
    resid_grad = lax.ppermute(landed_resid, both, home_turn(nz))
    stream_grad, resid_grad = lax.optimization_barrier((stream_grad, resid_grad))

    all_rows = lax.all_to_all(
        jnp.broadcast_to(stream_grad[None], (mp_count, tokens, block)), "mp", 0, 0, tiled=True
    )
    gate = pl.pallas_call(
        gate_kernel,
        in_specs=[pl.BlockSpec(memory_space=pltpu.VMEM)] * 3,
        out_specs=pl.BlockSpec(memory_space=pltpu.VMEM),
        out_shape=jax.ShapeDtypeStruct((dp_count, mp_count, per_expert * capacity), f32),
        compiler_params=pltpu.CompilerParams(vmem_limit_bytes=32 * 1024 * 1024),
    )(side_all, all_rows, proj)
    down_grad = pl.pallas_call(
        down_kernel,
        grid=(per_expert,),
        in_specs=[
            pl.BlockSpec((dp_count, per_expert, capacity, lanes), lambda e: (0, 0, 0, 0)),
            pl.BlockSpec((dp_count, tokens, block), lambda e: (0, 0, 0)),
            pl.BlockSpec((dp_count, 1, capacity, hidden_width), lambda e: (0, e, 0, 0)),
        ],
        out_specs=pl.BlockSpec((1, hidden_width, block), lambda e: (e, 0, 0)),
        out_shape=jax.ShapeDtypeStruct((per_expert, hidden_width, block), bf16),
        scratch_shapes=[pltpu.VMEM((per_expert, dp_count, capacity, block), bf16)],
        compiler_params=pltpu.CompilerParams(vmem_limit_bytes=56 * 1024 * 1024),
    )(side_all, all_rows, acts_all)

    gate = lax.all_to_all(
        gate.reshape(dp_count * mp_count, 1, per_expert * capacity), both, 0, 0, tiled=True
    ).reshape(dp_count, mp_count, per_expert * capacity)
    slot_gate = jnp.sum(gate, axis=0).reshape(experts_all, capacity)
    per_token = jnp.sum(jnp.where(matches, slot_gate[:, :, None], 0.0), axis=1)
    gate_grad = jnp.sum(jnp.where(hit_routes, per_token.T[:, None, :], 0.0), axis=2)
    return (resid_grad, down_grad, gate_grad)


def solution(mesh):
    placed = (
        P("dp", None),
        P(),
        P("dp", "mp"),
        P("dp"),
        P("dp"),
        P("dp"),
        P("dp"),
        P("dp", None),
        P("dp", None),
        P("mp", "dp", None, None),
        P("mp", None, "dp"),
    )
    return jax.shard_map(
        local,
        mesh=mesh,
        in_specs=placed,
        out_specs=(P("dp", "mp"), P("mp", None, "dp"), P("dp", None)),
        check_vma=False,
    )
```

```python
import functools

import jax
import jax.numpy as jnp
from jax import lax
from jax.experimental import pallas as pl
from jax.experimental.pallas import tpu as pltpu
from jax.sharding import PartitionSpec as P

clip_low = 0.8
clip_high = 1.2
norm_eps = 1e-06
f32 = jnp.float32
bf16 = jnp.bfloat16
lanes = 128


def z_shift(step, nz):
    return [(2 * z + c, 2 * ((z + step) % nz) + c) for z in range(nz) for c in range(2)]


def core_swap(nz):
    return [(2 * z + c, 2 * z + 1 - c) for z in range(nz) for c in range(2)]


def home_turn(nz):
    return [
        ((2 * z + c) * 16 + 2 * b + low, (2 * z + low) * 16 + 2 * b + c)
        for z in range(nz) for c in range(2) for b in range(nz) for low in range(2)
    ]


def sum_turn(nz):
    return [
        ((2 * z + c) * 16 + 2 * b + low, (2 * b + c) * 16 + 2 * z + low)
        for z in range(nz) for c in range(2) for b in range(nz) for low in range(2)
    ]


def proj_kernel(acts_ref, down_ref, proj_ref):
    groups, _, slots, wide = acts_ref.shape
    acts = acts_ref[:, 0].reshape(groups * slots, wide)
    out = jnp.dot(acts, down_ref[0], preferred_element_type=f32)
    proj_ref[...] = out.astype(proj_ref.dtype).reshape(proj_ref.shape)


def gate_kernel(side_ref, rows_ref, proj_ref, gate_ref):
    groups, per_expert, slots, _ = side_ref.shape
    tokens, width = rows_ref.shape[1:]
    count = per_expert * slots
    column = lax.broadcasted_iota(jnp.int32, (count, tokens), 1)
    gates = jnp.zeros((count, lanes), f32)
    for group in range(groups):
        token = side_ref[group].reshape(count, lanes)[:, 1:2].astype(f32)
        match = jnp.where(column.astype(f32) == token, 1.0, 0.0).astype(bf16)
        rows = jnp.dot(match, rows_ref[group], preferred_element_type=f32)
        gate = jnp.sum(rows * proj_ref[group].reshape(count, width), axis=1, keepdims=True)
        gates = jnp.where(column == group, gate, gates)
    gates = gates.T
    for group in range(groups):
        gate_ref[group] = jnp.broadcast_to(gates[group : group + 1], gate_ref.shape[1:])


def hidden_kernel(nz, place_ref, grad_ref, *refs):
    pieces, out_ref = refs[: nz + 1], refs[nz + 1]
    z_index, core = place_ref[0], place_ref[1]
    tokens = grad_ref.shape[0] // 2
    half = pieces[0].shape[0] // 2
    grad = grad_ref[...]
    for number in range(nz + 1):
        step = (number + 1) // 2
        offset = step if number % 2 == 0 else nz - step
        first = 0
        if number >= nz - 1:
            offset, first = nz // 2, half * (number - nz + 1)
        part = lax.dot_general(
            pieces[number][...], grad, (((1,), (1,)), ((), ())), preferred_element_type=f32
        ).astype(out_ref.dtype)
        rows = slice(first, first + part.shape[0])
        block = lax.rem(z_index + offset, nz)
        out_ref[2 * block + core, rows] = part[:, :tokens]
        out_ref[2 * block + 1 - core, rows] = part[:, tokens:]


def down_kernel(side_ref, rows_ref, acts_ref, out_ref, weighted):
    groups, per_expert, slots, _ = side_ref.shape
    tokens, width = rows_ref.shape[1:]
    count = per_expert * slots
    expert = pl.program_id(0)

    @pl.when(expert == 0)
    def _():
        column = lax.broadcasted_iota(jnp.int32, (count, tokens), 1).astype(f32)
        for group in range(groups):
            side = side_ref[group].reshape(count, lanes).astype(f32)
            match = jnp.where(column == side[:, 1:2], 1.0, 0.0).astype(bf16)
            rows = jnp.dot(match, rows_ref[group], preferred_element_type=f32)
            made = (side[:, 0:1] * rows).astype(bf16)
            weighted[:, group] = made.reshape(per_expert, slots, width)

    acts = acts_ref[:, 0].reshape(groups * slots, acts_ref.shape[3])
    out_ref[0] = lax.dot_general(
        acts,
        weighted[expert].reshape(groups * slots, width),
        (((0,), (0,)), ((), ())),
        preferred_element_type=f32,
    ).astype(bf16)


def local(
    residual,
    norm_gain,
    head_weight,
    token_ids,
    old_logp,
    advantages,
    resp_mask,
    routes,
    combine_weights,
    expert_acts,
    down_weight,
):
    tokens, model_width = residual.shape
    block, vocab_dev = head_weight.shape
    per_expert, _, capacity, hidden_width = expert_acts.shape
    dp_count = lax.axis_size("dp")
    mp_count = lax.axis_size("mp")
    nz = dp_count // 2
    dp_index = lax.axis_index("dp")
    mp_index = lax.axis_index("mp")
    z_index, core = dp_index // 2, dp_index % 2
    both = ("dp", "mp")
    experts_all = per_expert * mp_count
    swap = functools.partial(lax.ppermute, axis_name="dp", perm=core_swap(nz))

    stream = residual.astype(f32)
    inv_rms = lax.rsqrt(jnp.mean(stream * stream, axis=1, keepdims=True) + norm_eps)
    normed = (stream * inv_rms * norm_gain[None, :]).astype(bf16)
    by_block = normed.reshape(tokens, nz, 2, block).transpose(2, 1, 0, 3)
    mine = lax.dynamic_index_in_dim(by_block, core, 0, keepdims=False)
    theirs = lax.dynamic_index_in_dim(by_block, 1 - core, 0, keepdims=False)
    chip_normed = jnp.concatenate([mine, swap(theirs)], axis=1)

    low = mp_index % 2
    landed_block = mp_index - low + core
    other_stream = swap(
        lax.dynamic_slice_in_dim(residual, (mp_index - low + 1 - core) * block, block, 1)
    )
    landed_stream = jnp.where(
        low == core, lax.dynamic_slice_in_dim(residual, landed_block * block, block, 1), other_stream
    )

    expert_ids = jnp.arange(experts_all, dtype=jnp.int32)
    hit_routes = routes[:, :, None] == expert_ids[None, None, :]
    hit_token = jnp.sum(hit_routes.astype(jnp.int32), axis=1)
    before = jnp.cumsum(hit_token, axis=0) - hit_token
    slot_ids = jnp.arange(capacity, dtype=jnp.int32)
    matches = (hit_token.T[:, None, :] == 1) & (before.T[:, None, :] == slot_ids[None, :, None])
    weight_token = jnp.sum(
        jnp.where(hit_routes, combine_weights[:, :, None].astype(f32), 0.0), axis=1
    )
    first_expert = mp_index * per_expert
    own_matches = lax.dynamic_slice_in_dim(matches, first_expert, per_expert, 0)
    own_weights = lax.dynamic_slice_in_dim(weight_token, first_expert, per_expert, 1)
    token_numbers = jnp.arange(tokens, dtype=jnp.int32)
    slot_token = jnp.sum(jnp.where(own_matches, token_numbers[None, None, :] + 1, 0), axis=2) - 1
    slot_weight = jnp.sum(jnp.where(own_matches, own_weights.T[:, None, :], 0.0), axis=2)
    lane = jnp.arange(lanes, dtype=jnp.int32)
    side = jnp.where(
        lane == 0,
        slot_weight[:, :, None],
        jnp.where(lane == 1, slot_token.astype(f32)[:, :, None], 0.0),
    ).astype(bf16)
    acts_block = jnp.concatenate([expert_acts[:, 0], side], axis=2)

    def logits_of(rows, offset, first, piece):
        features = lax.dynamic_index_in_dim(
            chip_normed, lax.rem(z_index + offset, nz), 0, keepdims=False
        )[rows, first : first + piece.shape[0]]
        return jnp.dot(features, piece, preferred_element_type=f32)

    everything = slice(0, 2 * tokens)
    ahead = lax.ppermute(head_weight, "dp", z_shift(1, nz))
    back = lax.ppermute(head_weight, "dp", z_shift(-1, nz))
    head_pieces = [(0, 0, head_weight), (nz - 1, 0, ahead), (1, 0, back)]
    back, chip_normed, landed_stream, acts_block = lax.optimization_barrier(
        (back, chip_normed, landed_stream, acts_block)
    )
    partial, used = None, 0
    for step in range(2, nz // 2):
        if step > 2:
            back, partial = lax.optimization_barrier((back, partial))
        for piece in head_pieces[used:]:
            added = logits_of(everything, *piece)
            partial = added if partial is None else partial + added
        used = len(head_pieces)
        ahead = lax.ppermute(ahead, "dp", z_shift(1, nz))
        back = lax.ppermute(back, "dp", z_shift(-1, nz))
        head_pieces += [(nz - step, 0, ahead), (step, 0, back)]
    back, partial = lax.optimization_barrier((back, partial))
    half = block // 2
    last_pieces = [
        (nz // 2, 0, lax.ppermute(ahead[:half], "dp", z_shift(1, nz))),
        (nz // 2, half, lax.ppermute(back[half:], "dp", z_shift(-1, nz))),
    ]
    for piece in head_pieces[used:]:
        partial = partial + logits_of(everything, *piece)
    own_part, early = partial[:tokens], swap(partial[tokens:])
    late = None
    for piece in last_pieces:
        added = logits_of(slice(tokens, None), *piece)
        late = added if late is None else late + added
    late = swap(late)
    own_part = own_part + early
    for piece in last_pieces:
        own_part = own_part + logits_of(slice(0, tokens), *piece)
    head_pieces += last_pieces
    logits = own_part + late

    acts_block, _ = lax.optimization_barrier((acts_block, tuple(p for _, _, p in last_pieces)))
    acts_all = lax.all_gather(acts_block, "dp", axis=0, tiled=False)
    proj = pl.pallas_call(
        proj_kernel,
        grid=(per_expert,),
        in_specs=[
            pl.BlockSpec((dp_count, 1, capacity, hidden_width), lambda e: (0, e, 0, 0)),
            pl.BlockSpec((1, hidden_width, block), lambda e: (e, 0, 0)),
        ],
        out_specs=pl.BlockSpec((dp_count, 1, capacity, block), lambda e: (0, e, 0, 0)),
        out_shape=jax.ShapeDtypeStruct((dp_count, per_expert, capacity, block), f32),
        compiler_params=pltpu.CompilerParams(vmem_limit_bytes=58 * 1024 * 1024),
    )(acts_all, down_weight)

    local_ids = token_ids - mp_index * vocab_dev
    column = jnp.arange(vocab_dev, dtype=jnp.int32)
    onehot = column[None, :] == local_ids[:, None]
    local_top = jnp.max(logits, axis=1)
    local_exp = jnp.exp(logits - local_top[:, None])
    local_total = jnp.sum(local_exp, axis=1)
    local_mean = jnp.sum(local_exp * logits, axis=1)
    local_picked = jnp.sum(jnp.where(onehot, logits, 0.0), axis=1)
    stats = jnp.stack([local_top, local_total, local_mean, local_picked])
    stats = lax.all_to_all(
        jnp.broadcast_to(stats[None], (mp_count, 4, tokens)), "mp", 0, 0, tiled=True
    )
    row_top = jnp.max(stats[:, 0], axis=0)
    rescale = jnp.exp(stats[:, 0] - row_top[None])
    row_total = jnp.sum(stats[:, 1] * rescale, axis=0)
    mean_logit = jnp.sum(stats[:, 2] * rescale, axis=0) / row_total
    picked = jnp.sum(stats[:, 3], axis=0)

    logp = picked - row_top - jnp.log(row_total)
    prob_ratio = jnp.exp(logp - old_logp)
    weight_row = -jnp.clip(prob_ratio, clip_low, clip_high) * advantages * resp_mask.astype(f32)
    inner = weight_row * (picked - mean_logit) / model_width
    own_rows = jnp.stack([inv_rms[:, 0], inner])
    landed_rows = jnp.where(low == core, own_rows, swap(own_rows))
    logit_grad = (
        weight_row[:, None]
        * (onehot.astype(f32) - jnp.exp(logits - row_top[:, None]) / row_total[:, None])
    ).astype(bf16)
    chip_grad = jnp.concatenate([logit_grad, swap(logit_grad)], axis=0)

    place = jnp.stack([z_index, core]).astype(jnp.int32)
    hidden = pl.pallas_call(
        functools.partial(hidden_kernel, nz),
        in_specs=[pl.BlockSpec(memory_space=pltpu.SMEM)]
        + [pl.BlockSpec(memory_space=pltpu.VMEM)] * (nz + 2),
        out_specs=pl.BlockSpec(memory_space=pltpu.VMEM),
        out_shape=jax.ShapeDtypeStruct((mp_count, block, tokens), f32),
        compiler_params=pltpu.CompilerParams(vmem_limit_bytes=40 * 1024 * 1024),
    )(place, chip_grad, *[piece for _, _, piece in head_pieces])

    hidden = lax.all_to_all(hidden, "mp", 0, 0, tiled=True)
    side_all = acts_all[..., hidden_width:]
    hidden, proj, side_all, landed_rows = lax.optimization_barrier(
        (hidden, proj, side_all, landed_rows)
    )
    hidden_grad = jnp.sum(hidden, axis=0).T

    landed_gain = lax.dynamic_slice_in_dim(norm_gain, landed_block * block, block, 0)
    landed_rms, landed_inner = landed_rows[0][:, None], landed_rows[1][:, None]
    scaled_grad = landed_gain[None, :] * hidden_grad
    landed_resid = landed_rms * (
        scaled_grad - landed_stream.astype(f32) * landed_rms * landed_inner
    )
    stream_grad = lax.ppermute(landed_resid.astype(bf16), both, sum_turn(nz))
    resid_grad = lax.ppermute(landed_resid, both, home_turn(nz))
    stream_grad, resid_grad = lax.optimization_barrier((stream_grad, resid_grad))

    all_rows = lax.all_to_all(
        jnp.broadcast_to(stream_grad[None], (mp_count, tokens, block)), "mp", 0, 0, tiled=True
    )
    gate = pl.pallas_call(
        gate_kernel,
        in_specs=[pl.BlockSpec(memory_space=pltpu.VMEM)] * 3,
        out_specs=pl.BlockSpec(memory_space=pltpu.VMEM),
        out_shape=jax.ShapeDtypeStruct((dp_count, mp_count, per_expert * capacity), f32),
        compiler_params=pltpu.CompilerParams(vmem_limit_bytes=32 * 1024 * 1024),
    )(side_all, all_rows, proj)
    down_grad = pl.pallas_call(
        down_kernel,
        grid=(per_expert,),
        in_specs=[
            pl.BlockSpec((dp_count, per_expert, capacity, lanes), lambda e: (0, 0, 0, 0)),
            pl.BlockSpec((dp_count, tokens, block), lambda e: (0, 0, 0)),
            pl.BlockSpec((dp_count, 1, capacity, hidden_width), lambda e: (0, e, 0, 0)),
        ],
        out_specs=pl.BlockSpec((1, hidden_width, block), lambda e: (e, 0, 0)),
        out_shape=jax.ShapeDtypeStruct((per_expert, hidden_width, block), bf16),
        scratch_shapes=[pltpu.VMEM((per_expert, dp_count, capacity, block), bf16)],
        compiler_params=pltpu.CompilerParams(vmem_limit_bytes=56 * 1024 * 1024),
    )(side_all, all_rows, acts_all)

    gate = lax.all_to_all(
        gate.reshape(dp_count * mp_count, 1, per_expert * capacity), both, 0, 0, tiled=True
    ).reshape(dp_count, mp_count, per_expert * capacity)
    slot_gate = jnp.sum(gate, axis=0).reshape(experts_all, capacity)
    per_token = jnp.sum(jnp.where(matches, slot_gate[:, :, None], 0.0), axis=1)
    gate_grad = jnp.sum(jnp.where(hit_routes, per_token.T[:, None, :], 0.0), axis=2)
    return (resid_grad, down_grad, gate_grad)


def solution(mesh):
    placed = (
        P("dp", None),
        P(),
        P("dp", "mp"),
        P("dp"),
        P("dp"),
        P("dp"),
        P("dp"),
        P("dp", None),
        P("dp", None),
        P("mp", "dp", None, None),
        P("mp", None, "dp"),
    )
    return jax.shard_map(
        local,
        mesh=mesh,
        in_specs=placed,
        out_specs=(P("dp", "mp"), P("mp", None, "dp"), P("dp", None)),
        check_vma=False,
    )
```

```python
import functools

import jax
import jax.numpy as jnp
from jax import lax
from jax.experimental import pallas as pl
from jax.experimental.pallas import tpu as pltpu
from jax.sharding import PartitionSpec as P

clip_low = 0.8
clip_high = 1.2
norm_eps = 1e-06
f32 = jnp.float32
bf16 = jnp.bfloat16
lanes = 128


def z_shift(step, nz):
    return [(2 * z + c, 2 * ((z + step) % nz) + c) for z in range(nz) for c in range(2)]


def core_swap(nz):
    return [(2 * z + c, 2 * z + 1 - c) for z in range(nz) for c in range(2)]


def home_turn(nz):
    return [
        ((2 * z + c) * 16 + 2 * b + low, (2 * z + low) * 16 + 2 * b + c)
        for z in range(nz) for c in range(2) for b in range(nz) for low in range(2)
    ]


def sum_turn(nz):
    return [
        ((2 * z + c) * 16 + 2 * b + low, (2 * b + c) * 16 + 2 * z + low)
        for z in range(nz) for c in range(2) for b in range(nz) for low in range(2)
    ]


def proj_kernel(acts_ref, down_ref, proj_ref):
    groups, _, slots, wide = acts_ref.shape
    acts = acts_ref[:, 0].reshape(groups * slots, wide)
    out = jnp.dot(acts, down_ref[0], preferred_element_type=f32)
    proj_ref[...] = out.astype(proj_ref.dtype).reshape(proj_ref.shape)


def gate_kernel(side_ref, rows_ref, proj_ref, gate_ref):
    groups, per_expert, slots, _ = side_ref.shape
    tokens, width = rows_ref.shape[1:]
    count = per_expert * slots
    column = lax.broadcasted_iota(jnp.int32, (count, tokens), 1)
    gates = jnp.zeros((count, lanes), f32)
    for group in range(groups):
        token = side_ref[group].reshape(count, lanes)[:, 1:2].astype(f32)
        match = jnp.where(column.astype(f32) == token, 1.0, 0.0).astype(bf16)
        rows = jnp.dot(match, rows_ref[group], preferred_element_type=f32)
        gate = jnp.sum(rows * proj_ref[group].reshape(count, width), axis=1, keepdims=True)
        gates = jnp.where(column == group, gate, gates)
    gates = gates.T
    for group in range(groups):
        gate_ref[group] = jnp.broadcast_to(gates[group : group + 1], gate_ref.shape[1:])


def hidden_kernel(nz, place_ref, grad_ref, *refs):
    pieces, out_ref = refs[: nz + 1], refs[nz + 1]
    z_index, core = place_ref[0], place_ref[1]
    tokens = grad_ref.shape[0] // 2
    half = pieces[0].shape[0] // 2
    grad = grad_ref[...]
    for number in range(nz + 1):
        step = (number + 1) // 2
        offset = step if number % 2 == 0 else nz - step
        first = 0
        if number >= nz - 1:
            offset, first = nz // 2, half * (number - nz + 1)
        part = lax.dot_general(
            pieces[number][...], grad, (((1,), (1,)), ((), ())), preferred_element_type=f32
        ).astype(out_ref.dtype)
        rows = slice(first, first + part.shape[0])
        block = lax.rem(z_index + offset, nz)
        out_ref[2 * block + core, rows] = part[:, :tokens]
        out_ref[2 * block + 1 - core, rows] = part[:, tokens:]


def down_kernel(side_ref, rows_ref, acts_ref, out_ref, weighted):
    groups, per_expert, slots, _ = side_ref.shape
    tokens, width = rows_ref.shape[1:]
    count = per_expert * slots
    expert = pl.program_id(0)

    @pl.when(expert == 0)
    def _():
        column = lax.broadcasted_iota(jnp.int32, (count, tokens), 1).astype(f32)
        for group in range(groups):
            side = side_ref[group].reshape(count, lanes).astype(f32)
            match = jnp.where(column == side[:, 1:2], 1.0, 0.0).astype(bf16)
            rows = jnp.dot(match, rows_ref[group], preferred_element_type=f32)
            made = (side[:, 0:1] * rows).astype(bf16)
            weighted[:, group] = made.reshape(per_expert, slots, width)

    acts = acts_ref[:, 0].reshape(groups * slots, acts_ref.shape[3])
    out_ref[0] = lax.dot_general(
        acts,
        weighted[expert].reshape(groups * slots, width),
        (((0,), (0,)), ((), ())),
        preferred_element_type=f32,
    ).astype(bf16)


def local(
    residual,
    norm_gain,
    head_weight,
    token_ids,
    old_logp,
    advantages,
    resp_mask,
    routes,
    combine_weights,
    expert_acts,
    down_weight,
):
    tokens, model_width = residual.shape
    block, vocab_dev = head_weight.shape
    per_expert, _, capacity, hidden_width = expert_acts.shape
    dp_count = lax.axis_size("dp")
    mp_count = lax.axis_size("mp")
    nz = dp_count // 2
    dp_index = lax.axis_index("dp")
    mp_index = lax.axis_index("mp")
    z_index, core = dp_index // 2, dp_index % 2
    both = ("dp", "mp")
    experts_all = per_expert * mp_count
    swap = functools.partial(lax.ppermute, axis_name="dp", perm=core_swap(nz))

    stream = residual.astype(f32)
    inv_rms = lax.rsqrt(jnp.mean(stream * stream, axis=1, keepdims=True) + norm_eps)
    normed = (stream * inv_rms * norm_gain[None, :]).astype(bf16)
    by_block = normed.reshape(tokens, nz, 2, block).transpose(2, 1, 0, 3)
    mine = lax.dynamic_index_in_dim(by_block, core, 0, keepdims=False)
    theirs = lax.dynamic_index_in_dim(by_block, 1 - core, 0, keepdims=False)
    chip_normed = jnp.concatenate([mine, swap(theirs)], axis=1)

    low = mp_index % 2
    landed_block = mp_index - low + core
    other_stream = swap(
        lax.dynamic_slice_in_dim(residual, (mp_index - low + 1 - core) * block, block, 1)
    )
    landed_stream = jnp.where(
        low == core, lax.dynamic_slice_in_dim(residual, landed_block * block, block, 1), other_stream
    )

    expert_ids = jnp.arange(experts_all, dtype=jnp.int32)
    hit_routes = routes[:, :, None] == expert_ids[None, None, :]
    hit_token = jnp.sum(hit_routes.astype(jnp.int32), axis=1)
    before = jnp.cumsum(hit_token, axis=0) - hit_token
    slot_ids = jnp.arange(capacity, dtype=jnp.int32)
    matches = (hit_token.T[:, None, :] == 1) & (before.T[:, None, :] == slot_ids[None, :, None])
    weight_token = jnp.sum(
        jnp.where(hit_routes, combine_weights[:, :, None].astype(f32), 0.0), axis=1
    )
    first_expert = mp_index * per_expert
    own_matches = lax.dynamic_slice_in_dim(matches, first_expert, per_expert, 0)
    own_weights = lax.dynamic_slice_in_dim(weight_token, first_expert, per_expert, 1)
    token_numbers = jnp.arange(tokens, dtype=jnp.int32)
    slot_token = jnp.sum(jnp.where(own_matches, token_numbers[None, None, :] + 1, 0), axis=2) - 1
    slot_weight = jnp.sum(jnp.where(own_matches, own_weights.T[:, None, :], 0.0), axis=2)
    lane = jnp.arange(lanes, dtype=jnp.int32)
    side = jnp.where(
        lane == 0,
        slot_weight[:, :, None],
        jnp.where(lane == 1, slot_token.astype(f32)[:, :, None], 0.0),
    ).astype(bf16)
    acts_block = jnp.concatenate([expert_acts[:, 0], side], axis=2)

    def logits_of(rows, offset, first, piece):
        features = lax.dynamic_index_in_dim(
            chip_normed, lax.rem(z_index + offset, nz), 0, keepdims=False
        )[rows, first : first + piece.shape[0]]
        return jnp.dot(features, piece, preferred_element_type=f32)

    everything = slice(0, 2 * tokens)
    ahead = lax.ppermute(head_weight, "dp", z_shift(1, nz))
    back = lax.ppermute(head_weight, "dp", z_shift(-1, nz))
    head_pieces = [(0, 0, head_weight), (nz - 1, 0, ahead), (1, 0, back)]
    back, chip_normed, landed_stream, acts_block = lax.optimization_barrier(
        (back, chip_normed, landed_stream, acts_block)
    )
    partial, used = None, 0
    for step in range(2, nz // 2):
        if step > 2:
            back, partial = lax.optimization_barrier((back, partial))
        for piece in head_pieces[used:]:
            added = logits_of(everything, *piece)
            partial = added if partial is None else partial + added
        used = len(head_pieces)
        ahead = lax.ppermute(ahead, "dp", z_shift(1, nz))
        back = lax.ppermute(back, "dp", z_shift(-1, nz))
        head_pieces += [(nz - step, 0, ahead), (step, 0, back)]
    back, partial = lax.optimization_barrier((back, partial))
    half = block // 2
    last_pieces = [
        (nz // 2, 0, lax.ppermute(ahead[:half], "dp", z_shift(1, nz))),
        (nz // 2, half, lax.ppermute(back[half:], "dp", z_shift(-1, nz))),
    ]
    for piece in head_pieces[used:]:
        partial = partial + logits_of(everything, *piece)
    own_part, other_part = partial[:tokens], partial[tokens:]
    for piece in last_pieces:
        other_part = other_part + logits_of(slice(tokens, None), *piece)
        own_part = own_part + logits_of(slice(0, tokens), *piece)
    head_pieces += last_pieces
    logits = own_part + swap(other_part)

    acts_block, _ = lax.optimization_barrier(
        (acts_block, (partial,) + tuple(p for _, _, p in last_pieces))
    )
    acts_all = lax.all_gather(acts_block, "dp", axis=0, tiled=False)
    proj = pl.pallas_call(
        proj_kernel,
        grid=(per_expert,),
        in_specs=[
            pl.BlockSpec((dp_count, 1, capacity, hidden_width), lambda e: (0, e, 0, 0)),
            pl.BlockSpec((1, hidden_width, block), lambda e: (e, 0, 0)),
        ],
        out_specs=pl.BlockSpec((dp_count, 1, capacity, block), lambda e: (0, e, 0, 0)),
        out_shape=jax.ShapeDtypeStruct((dp_count, per_expert, capacity, block), f32),
        compiler_params=pltpu.CompilerParams(vmem_limit_bytes=58 * 1024 * 1024),
    )(acts_all, down_weight)

    local_ids = token_ids - mp_index * vocab_dev
    column = jnp.arange(vocab_dev, dtype=jnp.int32)
    onehot = column[None, :] == local_ids[:, None]
    local_top = jnp.max(logits, axis=1)
    local_exp = jnp.exp(logits - local_top[:, None])
    local_total = jnp.sum(local_exp, axis=1)
    local_mean = jnp.sum(local_exp * logits, axis=1)
    local_picked = jnp.sum(jnp.where(onehot, logits, 0.0), axis=1)
    stats = jnp.stack([local_top, local_total, local_mean, local_picked])
    stats = lax.all_to_all(
        jnp.broadcast_to(stats[None], (mp_count, 4, tokens)), "mp", 0, 0, tiled=True
    )
    row_top = jnp.max(stats[:, 0], axis=0)
    rescale = jnp.exp(stats[:, 0] - row_top[None])
    row_total = jnp.sum(stats[:, 1] * rescale, axis=0)
    mean_logit = jnp.sum(stats[:, 2] * rescale, axis=0) / row_total
    picked = jnp.sum(stats[:, 3], axis=0)

    logp = picked - row_top - jnp.log(row_total)
    prob_ratio = jnp.exp(logp - old_logp)
    weight_row = -jnp.clip(prob_ratio, clip_low, clip_high) * advantages * resp_mask.astype(f32)
    inner = weight_row * (picked - mean_logit) / model_width
    own_rows = jnp.stack([inv_rms[:, 0], inner])
    landed_rows = jnp.where(low == core, own_rows, swap(own_rows))
    logit_grad = (
        weight_row[:, None]
        * (onehot.astype(f32) - jnp.exp(logits - row_top[:, None]) / row_total[:, None])
    ).astype(bf16)
    chip_grad = jnp.concatenate([logit_grad, swap(logit_grad)], axis=0)

    place = jnp.stack([z_index, core]).astype(jnp.int32)
    hidden = pl.pallas_call(
        functools.partial(hidden_kernel, nz),
        in_specs=[pl.BlockSpec(memory_space=pltpu.SMEM)]
        + [pl.BlockSpec(memory_space=pltpu.VMEM)] * (nz + 2),
        out_specs=pl.BlockSpec(memory_space=pltpu.VMEM),
        out_shape=jax.ShapeDtypeStruct((mp_count, block, tokens), f32),
        compiler_params=pltpu.CompilerParams(vmem_limit_bytes=40 * 1024 * 1024),
    )(place, chip_grad, *[piece for _, _, piece in head_pieces])

    hidden = lax.all_to_all(hidden, "mp", 0, 0, tiled=True)
    side_all = acts_all[..., hidden_width:]
    hidden, proj, side_all, landed_rows = lax.optimization_barrier(
        (hidden, proj, side_all, landed_rows)
    )
    hidden_grad = jnp.sum(hidden, axis=0).T

    landed_gain = lax.dynamic_slice_in_dim(norm_gain, landed_block * block, block, 0)
    landed_rms, landed_inner = landed_rows[0][:, None], landed_rows[1][:, None]
    scaled_grad = landed_gain[None, :] * hidden_grad
    landed_resid = landed_rms * (
        scaled_grad - landed_stream.astype(f32) * landed_rms * landed_inner
    )
    stream_grad = lax.ppermute(landed_resid.astype(bf16), both, sum_turn(nz))
    resid_grad = lax.ppermute(landed_resid, both, home_turn(nz))
    stream_grad, resid_grad = lax.optimization_barrier((stream_grad, resid_grad))

    all_rows = lax.all_to_all(
        jnp.broadcast_to(stream_grad[None], (mp_count, tokens, block)), "mp", 0, 0, tiled=True
    )
    gate = pl.pallas_call(
        gate_kernel,
        in_specs=[pl.BlockSpec(memory_space=pltpu.VMEM)] * 3,
        out_specs=pl.BlockSpec(memory_space=pltpu.VMEM),
        out_shape=jax.ShapeDtypeStruct((dp_count, mp_count, per_expert * capacity), f32),
        compiler_params=pltpu.CompilerParams(vmem_limit_bytes=32 * 1024 * 1024),
    )(side_all, all_rows, proj)
    down_grad = pl.pallas_call(
        down_kernel,
        grid=(per_expert,),
        in_specs=[
            pl.BlockSpec((dp_count, per_expert, capacity, lanes), lambda e: (0, 0, 0, 0)),
            pl.BlockSpec((dp_count, tokens, block), lambda e: (0, 0, 0)),
            pl.BlockSpec((dp_count, 1, capacity, hidden_width), lambda e: (0, e, 0, 0)),
        ],
        out_specs=pl.BlockSpec((1, hidden_width, block), lambda e: (e, 0, 0)),
        out_shape=jax.ShapeDtypeStruct((per_expert, hidden_width, block), bf16),
        scratch_shapes=[pltpu.VMEM((per_expert, dp_count, capacity, block), bf16)],
        compiler_params=pltpu.CompilerParams(vmem_limit_bytes=56 * 1024 * 1024),
    )(side_all, all_rows, acts_all)

    gate = lax.all_to_all(
        gate.reshape(dp_count * mp_count, 1, per_expert * capacity), both, 0, 0, tiled=True
    ).reshape(dp_count, mp_count, per_expert * capacity)
    slot_gate = jnp.sum(gate, axis=0).reshape(experts_all, capacity)
    per_token = jnp.sum(jnp.where(matches, slot_gate[:, :, None], 0.0), axis=1)
    gate_grad = jnp.sum(jnp.where(hit_routes, per_token.T[:, None, :], 0.0), axis=2)
    return (resid_grad, down_grad, gate_grad)


def solution(mesh):
    placed = (
        P("dp", None),
        P(),
        P("dp", "mp"),
        P("dp"),
        P("dp"),
        P("dp"),
        P("dp"),
        P("dp", None),
        P("dp", None),
        P("mp", "dp", None, None),
        P("mp", None, "dp"),
    )
    return jax.shard_map(
        local,
        mesh=mesh,
        in_specs=placed,
        out_specs=(P("dp", "mp"), P("mp", None, "dp"), P("dp", None)),
        check_vma=False,
    )
```
